256 devices in a mesh: src: 64 (over y, x, z_hi, core), tgt: 4 (over z_lo).
Axes of the slice: x: 4, y: 4, z: 8 (z_hi: 2, z_lo: 4; z = z_hi * 4 + z_lo), core: 2. Of those that a mesh axis runs over, the one named last changes fastest.
Arguments:
- sources: bfloat16 [65536, 1024], P('src'), may hold values from -16 to 16
- targets: bfloat16 [8192, 1024], P(('src', 'tgt')), may hold values from -40 to 40
Outputs:
- row_best: float32 [65536], P('src')
- col_best: float32 [8192], P(('src', 'tgt'))
The draws below stay inside these ranges and needn't reach their ends.
All inputs are finite; a program needn't handle non-finite values.
Results may differ from the reference program's by a relative error of at most 0.00096.
Values may be sent and summed in bfloat16 or wider, within the bound.
A program may use at most 64 MiB of HBM per device.

```python
import math
import jax
import jax.numpy as jnp
from jax import lax

D = 1024
S = 65536
TGT = 8192


def shared_sources(key):
    return jnp.clip(jax.random.normal(key, (S, D), jnp.float32), -4.0, 4.0)


def draw_sources(key, part):
    base = shared_sources(key)
    return base.astype(jnp.bfloat16)


def draw_targets(key, part):
    base = shared_sources(key)
    key = jax.random.fold_in(key, 5)
    partner = jax.random.randint(jax.random.fold_in(key, 1), (TGT,), 0, S)
    strength = jax.random.uniform(jax.random.fold_in(key, 2), (TGT, 1), jnp.float32, 0.0, 1.5)
    noise = jnp.clip(jax.random.normal(jax.random.fold_in(key, 4), (TGT, D), jnp.float32), -4.0, 4.0)
    mixed = strength * base[partner] + noise
    return mixed.astype(jnp.bfloat16)


def setup_inputs(seed: int = 0) -> dict:
    key_list = jax.random.split(jax.random.key(seed), 3)
    return {
        "sources": draw_sources(jax.random.fold_in(key_list[2], 71), 0),
        "targets": draw_targets(jax.random.fold_in(key_list[2], 71), 0),
    }


sharpness_factor = 0.05

def unit_rows(matrix):
    values = matrix.astype(jnp.float32)
    scale = lax.rsqrt(lax.optimization_barrier(jnp.mean(values * values, axis=1, keepdims=True)) + 1e-06)
    return (values * scale / math.sqrt(matrix.shape[1])).astype(jnp.bfloat16)

def reference(sources, targets):
    query_direction_list = unit_rows(sources)
    target_unit = unit_rows(targets)
    total_src = query_direction_list.shape[0]
    total_tgt = target_unit.shape[0]
    stride = math.gcd(total_src, 1024)
    blocks = query_direction_list.reshape(total_src // stride, stride, query_direction_list.shape[1])

    def first_pass(col_totals, source_block):
        angular_agreement = jnp.dot(source_block, target_unit.T, preferred_element_type=jnp.float32)
        nearby_shares = jnp.exp(angular_agreement / sharpness_factor)
        return (col_totals + lax.optimization_barrier(jnp.sum(nearby_shares, axis=0)), lax.optimization_barrier(jnp.sum(nearby_shares, axis=1)))
    col_totals, row_totals = lax.scan(first_pass, jnp.zeros((total_tgt,), jnp.float32), blocks)
    left_side_divisor = jnp.log(row_totals / total_tgt)
    target_side_divisor = jnp.log(col_totals / total_src)

    def second_pass(col_top, inputs):
        source_block, left_entry_group = inputs
        angular_agreement = jnp.dot(source_block, target_unit.T, preferred_element_type=jnp.float32)
        ratio_criterion = angular_agreement - 0.5 * sharpness_factor * (left_entry_group[:, None] + target_side_divisor[None, :])
        return (jnp.maximum(col_top, lax.optimization_barrier(jnp.max(ratio_criterion, axis=0))), lax.optimization_barrier(jnp.max(ratio_criterion, axis=1)))
    start_top = jnp.full((total_tgt,), -1e+30, jnp.float32)
    col_best, row_best = lax.scan(second_pass, start_top, (blocks, left_side_divisor))
    return (row_best.reshape(total_src), col_best)
```

```python
import functools
import math

import jax
import jax.numpy as jnp
from jax import lax
from jax.experimental import pallas as pl
from jax.experimental.pallas import tpu as pltpu
from jax.sharding import PartitionSpec as P

MESH = pl.DeviceIdType.MESH
EXP_SCALE = 20.0 * math.log2(math.e)
HALF = 0.025
RING = 4
ROWS, DEPTH, PIECE = 1024, 1024, 32
LANES = 128
ORDER = ((0, 0), (0, -1), (0, 1), (1, 0), (0, 2), (1, -1), (1, 1), (1, 2))
VIA_PLUS = ((0, 1), (-1, 2))


def unit_rows(values):
    values = values.astype(jnp.float32)
    scale = lax.rsqrt(jnp.mean(values * values, axis=1, keepdims=True) + 1e-06)
    return (values * scale * (1.0 / 32.0)).astype(jnp.bfloat16)


def kernel(
    src_ref,
    tgt_ref,
    row_ref,
    col_ref,
    unit,
    piece,
    gathered,
    cosine,
    row_acc,
    row_bias,
    col_part,
    col_one,
    col_two,
    max_one,
    max_two,
    row_one,
    row_max,
    col_norm,
    row_norm,
    load_sem,
    recv_sem,
    pair_sem,
    send_sem,
    small_send,
    small_recv,
):
    s = lax.axis_index("src")
    t = lax.axis_index("tgt")
    c = s % 2
    zh = (s // 2) % 2
    x = (s // 4) % 4
    y = s // 16
    a = x + c * (y - x)
    b = y + c * (x - y)

    def device(y, x, zh, c, t):
        return (((y * 4 + x) * 2 + zh) * 2 + c, t)

    def moved(da, db):
        aa, bb = (a + da + RING) % RING, (b + db + RING) % RING
        return device(bb + c * (aa - bb), aa + c * (bb - aa), zh, c, t)

    other_core = device(y, x, zh, 1 - c, t)
    other_plane = device(y, x, 1 - zh, c, 3 - t)

    load = pltpu.make_async_copy(src_ref, unit, load_sem.at[0])
    load.start()
    load_piece = pltpu.make_async_copy(tgt_ref, piece, load_sem.at[1])
    load_piece.start()

    me_one, me_two = x * 2 + c, y * 2 + zh
    peers_one, peers_two, peers_row = [], [], []
    for i in range(1, 8):
        p = (me_one + i) % 8
        peers_one.append(device(y, p // 2, zh, p % 2, t))
        p = (me_two + i) % 8
        q = p % 2
        other = (q - zh) * (q - zh)
        peers_two.append(device(p // 2, x, q, c, t + other * (3 - 2 * t)))
    for i in range(1, 4):
        peers_row.append(device(y, x, zh, c, (t + i) % 4))

    barrier = pltpu.get_barrier_semaphore()
    for peer in peers_one + peers_two + peers_row:
        pl.semaphore_signal(barrier, inc=1, device_id=peer, device_id_type=MESH)

    def plane_of(p):
        return zh if p == 0 else 1 - zh

    def ring(v, d):
        return (v + d + RING) % RING

    load_piece.wait()
    gathered[c, zh, b, a] = unit_rows(piece[...])
    pl.semaphore_wait(barrier, 17)

    sends = []

    def chunk_copy(p, db, da, to, send):
        pp, bb, aa = plane_of(p), ring(b, db), ring(a, da)
        slot = gathered.at[c, pp, bb, aa]
        return pltpu.make_async_remote_copy(
            src_ref=slot,
            dst_ref=slot,
            send_sem=send_sem.at[send],
            recv_sem=recv_sem.at[(pp * RING + bb) * RING + aa],
            device_id=to,
            device_id_type=MESH,
        )

    def forward(p, db, da, to):
        copy = chunk_copy(p, db, da, to, len(sends))
        copy.start()
        sends.append(copy)

    def arrived(p, db, da):
        chunk_copy(p, db, da, other_core, 0).wait_recv()

    def pair_copy(step, mine):
        p, db = ORDER[step]
        core = c if mine else 1 - c
        slot = gathered.at[core, plane_of(p), ring(b if mine else a, db)]
        return pltpu.make_async_remote_copy(
            src_ref=slot,
            dst_ref=slot,
            send_sem=send_sem.at[31 + step],
            recv_sem=pair_sem.at[step],
            device_id=other_core,
            device_id_type=MESH,
        )

    plus_a, minus_a, plus_b, minus_b = moved(1, 0), moved(-1, 0), moved(0, 1), moved(0, -1)

    def spread(step):
        p, db = ORDER[step]
        for da in (0, -1, 1, 2):
            if (p, db, da) != (0, 0, 0):
                arrived(p, db, da)
            if db == 0:
                if da == 0:
                    forward(p, 0, 0, plus_a)
                    forward(p, 0, 0, minus_a)
                    if p == 0:
                        forward(p, 0, 0, other_plane)
                if da == -1 and p == 0:
                    forward(p, 0, da, plus_a)
                if da == 1 and p == 1:
                    forward(p, 0, da, minus_a)
                forward(p, 0, da, plus_b)
                forward(p, 0, da, minus_b)
            elif db == -1 and da in VIA_PLUS[p]:
                forward(p, db, da, plus_b)
            elif db == 1 and da not in VIA_PLUS[p]:
                forward(p, db, da, minus_b)
            if (p, db, da) == (0, 0, 0):
                prepare()
        copy = pair_copy(step, True)
        copy.start()
        return copy

    def prepare():
        load.wait()

        def body(i, carry):
            rows = pl.ds(pl.multiple_of(i * 64, 64), 64)
            unit[rows, :] = unit_rows(unit[rows, :])
            return carry

        lax.fori_loop(0, ROWS // 64, body, 0)
        row_acc[...] = jnp.zeros_like(row_acc)

    def lines(step):
        p, db = ORDER[step]
        pp = plane_of(p)
        return (c * 2 + pp) * 4 + ring(b, db), ((1 - c) * 2 + pp) * 4 + ring(a, db)

    def multiply(step):
        p, db = ORDER[step]
        pair_copy(step, False).wait_recv()
        pp = plane_of(p)
        group = jnp.concatenate(
            [
                gathered[c, pp, ring(b, db)].reshape(LANES, DEPTH),
                gathered[1 - c, pp, ring(a, db)].reshape(LANES, DEPTH),
            ],
            axis=0,
        )
        mine, theirs = lines(step)
        block = 512

        def body(i, total):
            rows = pl.ds(pl.multiple_of(i * block, block), block)
            angle = lax.dot_general(
                unit[rows, :], group, (((1,), (1,)), ((), ())), preferred_element_type=jnp.float32
            )
            cosine[step, rows, :] = angle
            share = jnp.exp2(angle * EXP_SCALE)
            row_acc[rows, :] += share[:, :LANES] + share[:, LANES:]
            return total + jnp.sum(share.reshape(block // 8, 8, 2 * LANES), axis=0)

        total = lax.fori_loop(0, ROWS // block, body, jnp.zeros((8, 2 * LANES), jnp.float32))
        col_part[mine] = total[:, :LANES]
        col_part[theirs] = total[:, LANES:]

    pair_sends = [spread(0), spread(1)]
    for step in range(8):
        if step + 2 < 8:
            pair_sends.append(spread(step + 2))
        multiply(step)

    small = []

    def exchange(buffer, me, peers, base, width):
        for i, peer in enumerate(peers):
            copy = pltpu.make_async_remote_copy(
                src_ref=buffer.at[me],
                dst_ref=buffer.at[me],
                send_sem=small_send.at[base + i],
                recv_sem=small_recv.at[base + i],
                device_id=peer,
                device_id_type=MESH,
            )
            copy.start()
            small.append(copy)

    def collect(buffer, me, count, base, width):
        for i in range(count):
            slot = buffer.at[(me + width - 1 - i) % width]
            pltpu.make_async_remote_copy(
                src_ref=slot,
                dst_ref=slot,
                send_sem=small_send.at[base + i],
                recv_sem=small_recv.at[base + i],
                device_id=other_core,
                device_id_type=MESH,
            ).wait_recv()

    def columns(reduce, source):
        return reduce(source[...], axis=1)

    def rows_of(source, reduce):
        parts = []
        for i in range(8):
            block = source[i * LANES : (i + 1) * LANES, :]
            parts.append(reduce(block.T, axis=0, keepdims=True))
        return jnp.concatenate(parts, axis=0)

    col_one[me_one] = columns(jnp.sum, col_part)
    exchange(col_one, me_one, peers_one, 0, 8)
    row_one[t] = rows_of(row_acc, jnp.sum)
    exchange(row_one, t, peers_row, 14, 4)
    collect(col_one, me_one, 7, 0, 8)
    col_two[me_two] = jnp.sum(col_one[...], axis=0)
    exchange(col_two, me_two, peers_two, 7, 8)

    collect(row_one, t, 3, 14, 4)
    row_norm[...] = HALF * jnp.log(jnp.sum(row_one[...], axis=0) * (1.0 / 8192.0))
    for i in range(8):
        line = jnp.broadcast_to(row_norm[i : i + 1, :], (LANES, LANES))
        row_bias[i * LANES : (i + 1) * LANES, :] = line.T

    def col_body(i, tops):
        rows = pl.ds(pl.multiple_of(i * 32, 32), 32)
        bias = row_bias[rows, :]
        bias = jnp.concatenate([bias, bias], axis=1)
        new = []
        for step in range(8):
            value = (cosine[step, rows, :] - bias).reshape(4, 8, 2 * LANES)
            new.append(jnp.maximum(tops[step], jnp.max(value, axis=0)))
        return tuple(new)

    start = jnp.full((8, 2 * LANES), -1e30, jnp.float32)
    tops = lax.fori_loop(0, ROWS // 32, col_body, (start,) * 8)
    for step in range(8):
        mine, theirs = lines(step)
        col_part[mine] = tops[step][:, :LANES]
        col_part[theirs] = tops[step][:, LANES:]
    max_one[me_one] = columns(jnp.max, col_part)
    exchange(max_one, me_one, peers_one, 17, 8)

    collect(col_two, me_two, 7, 7, 8)
    col_norm[...] = HALF * jnp.log(jnp.sum(col_two[...], axis=0) * (1.0 / 65536.0))

    def row_body(i, carry):
        rows = pl.ds(pl.multiple_of(i * 32, 32), 32)
        top = None
        for step in range(8):
            mine, theirs = lines(step)
            value = cosine[step, rows, :]
            for part, line in ((value[:, :LANES], mine), (value[:, LANES:], theirs)):
                part = part - col_norm[pl.ds(line, 1), :]
                top = part if top is None else jnp.maximum(top, part)
        row_acc[rows, :] = top
        return carry

    lax.fori_loop(0, ROWS // 32, row_body, 0)
    row_max[t] = rows_of(row_acc, jnp.max)
    exchange(row_max, t, peers_row, 31, 4)

    collect(max_one, me_one, 7, 17, 8)
    max_two[me_two] = jnp.max(max_one[...], axis=0)
    exchange(max_two, me_two, peers_two, 24, 8)
    collect(row_max, t, 3, 31, 4)
    row_ref[...] = jnp.max(row_max[...], axis=0) - row_norm[...]
    collect(max_two, me_two, 7, 24, 8)
    best = jnp.max(max_two[...], axis=0) - col_norm[...]
    line = (c * 2 + zh) * 4 + b
    chosen = lax.broadcasted_iota(jnp.int32, (16, LANES), 0) == line
    best = jnp.sum(jnp.where(chosen, best, 0.0), axis=0, keepdims=True)
    out = jnp.zeros((1, PIECE), jnp.float32)
    for i in range(RING):
        out = jnp.where(a == i, best[:, i * PIECE : (i + 1) * PIECE], out)
    col_ref[...] = out

    for copy in sends + pair_sends + small:
        copy.wait_send()


def local(sources, targets):
    f32, bf16 = jnp.float32, jnp.bfloat16
    dma = pltpu.SemaphoreType.DMA
    row_best, col_best = pl.pallas_call(
        kernel,
        out_shape=(
            jax.ShapeDtypeStruct((8, LANES), f32),
            jax.ShapeDtypeStruct((1, PIECE), f32),
        ),
        in_specs=[pl.BlockSpec(memory_space=pl.ANY)] * 2,
        out_specs=(pl.BlockSpec(memory_space=pltpu.VMEM),) * 2,
        scratch_shapes=[
            pltpu.VMEM((ROWS, DEPTH), bf16),
            pltpu.VMEM((PIECE, DEPTH), bf16),
            pltpu.VMEM((2, 2, RING, RING, PIECE, DEPTH), bf16),
            pltpu.VMEM((8, ROWS, 2 * LANES), f32),
            pltpu.VMEM((ROWS, LANES), f32),
            pltpu.VMEM((ROWS, LANES), f32),
            pltpu.VMEM((16, 8, LANES), f32),
            pltpu.VMEM((8, 16, LANES), f32),
            pltpu.VMEM((8, 16, LANES), f32),
            pltpu.VMEM((8, 16, LANES), f32),
            pltpu.VMEM((8, 16, LANES), f32),
            pltpu.VMEM((4, 8, LANES), f32),
            pltpu.VMEM((4, 8, LANES), f32),
            pltpu.VMEM((16, LANES), f32),
            pltpu.VMEM((8, LANES), f32),
            dma((2,)),
            dma((32,)),
            dma((8,)),
            dma((39,)),
            dma((34,)),
            dma((34,)),
        ],
        compiler_params=pltpu.CompilerParams(
            collective_id=0, has_side_effects=True, vmem_limit_bytes=48 * 1024 * 1024
        ),
        cost_estimate=pl.CostEstimate(
            flops=2 * ROWS * 2048 * DEPTH, bytes_accessed=1 << 22, transcendentals=1 << 21
        ),
    )(sources, targets)
    return row_best.reshape(ROWS), col_best.reshape(PIECE)


def solution(mesh):
    in_specs = (P("src", None), P(("src", "tgt"), None))
    out_specs = (P("src"), P(("src", "tgt")))
    return jax.shard_map(local, mesh=mesh, in_specs=in_specs, out_specs=out_specs, check_vma=False)
```

```python
import functools
import math

import jax
import jax.numpy as jnp
from jax import lax
from jax.experimental import pallas as pl
from jax.experimental.pallas import tpu as pltpu
from jax.sharding import PartitionSpec as P

MESH = pl.DeviceIdType.MESH
EXP_SCALE = 20.0 * math.log2(math.e)
HALF = 0.025
RING = 4
ROWS, DEPTH, PIECE = 1024, 1024, 32
LANES = 128
ORDER = ((0, 0), (0, -1), (0, 1), (1, 0), (0, 2), (1, -1), (1, 1), (1, 2))


def plan():
    todo = []

    def send(plane, step_b, step_a, *ways):
        todo.extend(("send", plane, step_b, step_a, way) for way in ways)

    def take(plane, step_b, step_a, *ways):
        todo.append(("take", plane, step_b, step_a))
        send(plane, step_b, step_a, *ways)

    def share(*steps):
        todo.extend(("share", step) for step in steps)

    def multiply(*steps):
        todo.extend(("multiply", step) for step in steps)

    send(0, 0, 0, "z", "+a", "-a", "2a", "+b", "-b")
    todo.append(("prepare",))
    take(0, 0, -1, "+b", "-b")
    take(0, 0, 1, "+b", "-b")
    take(1, 0, 0, "+a", "-a", "2a")
    take(0, 0, 2, "+b", "-b")
    share(0)
    send(1, 0, 0, "+b", "-b", "2b")
    for d in (0, -1, 1, 2):
        take(0, -1, d, *(("+b",) if d in (0, 1) else ()))
        take(0, 1, d, *(() if d in (0, 1) else ("-b",)))
    share(1, 2)
    take(1, 0, -1, "+b", "-b")
    take(1, 0, 1, "+b", "-b")
    take(1, 0, 2, "+b", "-b")
    for d in (-1, 1, 2):
        send(1, 0, d, "2b")
    share(3)
    multiply(0, 1, 2)
    for d in (0, -1, 1, 2):
        take(0, 2, d)
    share(4)
    multiply(3)
    for d in (0, -1, 1, 2):
        take(1, -1, d)
        take(1, 1, d)
    share(5, 6)
    multiply(4)
    for d in (0, -1, 1, 2):
        take(1, 2, d)
    share(7)
    multiply(5, 6, 7)
    return todo


def unit_rows(values):
    values = values.astype(jnp.float32)
    scale = lax.rsqrt(jnp.mean(values * values, axis=1, keepdims=True) + 1e-06)
    return (values * scale * (1.0 / 32.0)).astype(jnp.bfloat16)


def kernel(
    src_ref,
    tgt_ref,
    row_ref,
    col_ref,
    unit,
    piece,
    gathered,
    cosine,
    row_acc,
    row_bias,
    col_part,
    col_one,
    col_two,
    col_top,
    best_of,
    row_one,
    row_max,
    col_norm,
    row_norm,
    load_sem,
    recv_sem,
    pair_sem,
    send_sem,
    small_send,
    small_recv,
    top_sem,
):
    s = lax.axis_index("src")
    t = lax.axis_index("tgt")
    c = s % 2
    zh = (s // 2) % 2
    x = (s // 4) % 4
    y = s // 16
    a = x + c * (y - x)
    b = y + c * (x - y)

    def device(y, x, zh, c, t):
        return (((y * 4 + x) * 2 + zh) * 2 + c, t)

    def moved(da, db):
        aa, bb = (a + da + RING) % RING, (b + db + RING) % RING
        return device(bb + c * (aa - bb), aa + c * (bb - aa), zh, c, t)

    other_core = device(y, x, zh, 1 - c, t)
    other_plane = device(y, x, 1 - zh, c, (t + 2) % 4)

    load = pltpu.make_async_copy(src_ref, unit, load_sem.at[0])
    load.start()
    load_piece = pltpu.make_async_copy(tgt_ref, piece, load_sem.at[1])
    load_piece.start()

    me_one, me_two = x * 2 + c, y * 2 + zh
    peers_one, peers_two, peers_row = [], [], []
    for i in range(1, 8):
        p = (me_one + i) % 8
        peers_one.append(device(y, p // 2, zh, p % 2, t))
        p = (me_two + i) % 8
        q = p % 2
        other = (q - zh) * (q - zh)
        peers_two.append(device(p // 2, x, q, c, (t + other * 2) % 4))
    for i in range(1, 4):
        peers_row.append(device(y, x, zh, c, (t + i) % 4))

    barrier = pltpu.get_barrier_semaphore()
    greeted = [moved(1, 0), moved(2, 0), moved(3, 0), moved(0, 1), moved(0, 2), moved(0, 3), other_core, other_plane]
    greeted += peers_row
    for peer in greeted:
        pl.semaphore_signal(barrier, inc=1, device_id=peer, device_id_type=MESH)

    def plane_of(p):
        return zh if p == 0 else 1 - zh

    def ring(v, d):
        return (v + d + RING) % RING

    load_piece.wait()
    gathered[c, zh, b, a] = unit_rows(piece[...])
    pl.semaphore_wait(barrier, len(greeted))

    sends = []

    def chunk_copy(p, db, da, to, send):
        pp, bb, aa = plane_of(p), ring(b, db), ring(a, da)
        slot = gathered.at[c, pp, bb, aa]
        return pltpu.make_async_remote_copy(
            src_ref=slot,
            dst_ref=slot,
            send_sem=send_sem.at[send],
            recv_sem=recv_sem.at[(pp * RING + bb) * RING + aa],
            device_id=to,
            device_id_type=MESH,
        )

    def forward(p, db, da, to):
        copy = chunk_copy(p, db, da, to, len(sends))
        copy.start()
        sends.append(copy)

    def arrived(p, db, da):
        chunk_copy(p, db, da, other_core, 0).wait_recv()

    def pair_copy(step, mine):
        p, db = ORDER[step]
        core = c if mine else 1 - c
        slot = gathered.at[core, plane_of(p), ring(b if mine else a, db)]
        return pltpu.make_async_remote_copy(
            src_ref=slot,
            dst_ref=slot,
            send_sem=send_sem.at[31 + step],
            recv_sem=pair_sem.at[step],
            device_id=other_core,
            device_id_type=MESH,
        )

    plus_a, minus_a, plus_b, minus_b = moved(1, 0), moved(-1, 0), moved(0, 1), moved(0, -1)

    ways = {
        "+a": plus_a,
        "-a": minus_a,
        "2a": moved(2, 0),
        "+b": plus_b,
        "-b": minus_b,
        "2b": moved(0, 2),
        "z": other_plane,
    }

    def share(step):
        copy = pair_copy(step, True)
        copy.start()
        pair_sends.append(copy)

    def prepare():
        load.wait()

        def body(i, carry):
            rows = pl.ds(pl.multiple_of(i * 64, 64), 64)
            unit[rows, :] = unit_rows(unit[rows, :])
            return carry

        lax.fori_loop(0, ROWS // 64, body, 0)
        row_acc[...] = jnp.zeros_like(row_acc)

    def lines(step):
        p, db = ORDER[step]
        pp = plane_of(p)
        return (c * 2 + pp) * 4 + ring(b, db), ((1 - c) * 2 + pp) * 4 + ring(a, db)

    def multiply(step):
        p, db = ORDER[step]
        pair_copy(step, False).wait_recv()
        pp = plane_of(p)
        group = jnp.concatenate(
            [
                gathered[c, pp, ring(b, db)].reshape(LANES, DEPTH),
                gathered[1 - c, pp, ring(a, db)].reshape(LANES, DEPTH),
            ],
            axis=0,
        )
        mine, theirs = lines(step)
        block = 512

        def body(i, total):
            rows = pl.ds(pl.multiple_of(i * block, block), block)
            angle = lax.dot_general(
                unit[rows, :], group, (((1,), (1,)), ((), ())), preferred_element_type=jnp.float32
            )
            cosine[step, rows, :] = angle
            share = jnp.exp2(angle * EXP_SCALE)
            row_acc[rows, :] += share[:, :LANES] + share[:, LANES:]
            return total + jnp.sum(share.reshape(block // 8, 8, 2 * LANES), axis=0)

        total = lax.fori_loop(0, ROWS // block, body, jnp.zeros((8, 2 * LANES), jnp.float32))
        col_part[mine] = total[:, :LANES]
        col_part[theirs] = total[:, LANES:]

    pair_sends = []
    for event, *at in plan():
        if event == "take":
            arrived(*at)
        elif event == "send":
            forward(*at[:3], ways[at[3]])
        elif event == "share":
            share(*at)
        elif event == "multiply":
            multiply(*at)
        else:
            prepare()

    small = []

    def exchange(buffer, me, peers, base, width):
        for i, peer in enumerate(peers):
            copy = pltpu.make_async_remote_copy(
                src_ref=buffer.at[me],
                dst_ref=buffer.at[me],
                send_sem=small_send.at[base + i],
                recv_sem=small_recv.at[base + i],
                device_id=peer,
                device_id_type=MESH,
            )
            copy.start()
            small.append(copy)

    def collect(buffer, me, count, base, width):
        for i in range(count):
            slot = buffer.at[(me + width - 1 - i) % width]
            pltpu.make_async_remote_copy(
                src_ref=slot,
                dst_ref=slot,
                send_sem=small_send.at[base + i],
                recv_sem=small_recv.at[base + i],
                device_id=other_core,
                device_id_type=MESH,
            ).wait_recv()

    def columns(reduce, source):
        return reduce(source[...], axis=1)

    def rows_of(source, reduce):
        parts = []
        for i in range(8):
            block = source[i * LANES : (i + 1) * LANES, :]
            parts.append(reduce(block.T, axis=0, keepdims=True))
        return jnp.concatenate(parts, axis=0)

    col_one[me_one] = columns(jnp.sum, col_part)
    exchange(col_one, me_one, peers_one, 0, 8)
    row_one[t] = rows_of(row_acc, jnp.sum)
    exchange(row_one, t, peers_row, 14, 4)
    collect(col_one, me_one, 7, 0, 8)
    col_two[me_two] = jnp.sum(col_one[...], axis=0)
    exchange(col_two, me_two, peers_two, 7, 8)

    collect(row_one, t, 3, 14, 4)
    row_norm[...] = HALF * jnp.log(jnp.sum(row_one[...], axis=0) * (1.0 / 8192.0))
    for i in range(8):
        line = jnp.broadcast_to(row_norm[i : i + 1, :], (LANES, LANES))
        row_bias[i * LANES : (i + 1) * LANES, :] = line.T

    def col_body(i, tops):
        rows = pl.ds(pl.multiple_of(i * 32, 32), 32)
        bias = row_bias[rows, :]
        bias = jnp.concatenate([bias, bias], axis=1)
        new = []
        for step in range(8):
            value = (cosine[step, rows, :] - bias).reshape(4, 8, 2 * LANES)
            new.append(jnp.maximum(tops[step], jnp.max(value, axis=0)))
        return tuple(new)

    start = jnp.full((8, 2 * LANES), -1e30, jnp.float32)
    tops = lax.fori_loop(0, ROWS // 32, col_body, (start,) * 8)
    for step in range(8):
        mine, theirs = lines(step)
        col_part[mine] = tops[step][:, :LANES]
        col_part[theirs] = tops[step][:, LANES:]
    col_top[...] = jnp.max(col_part[...], axis=1, keepdims=True)
    me_all = (me_two // 2 * 4 + x) * 4 + zh * 2 + c
    best_of[me_all] = col_top[(c * 2 + zh) * 4 + b]

    def top_copy(i):
        p = (me_all + i) % 64
        qc, qz, qx, qy = p % 2, (p // 2) % 2, (p // 4) % 4, p // 16
        crossed = (qz - zh) * (qz - zh)
        return pltpu.make_async_remote_copy(
            src_ref=col_top.at[(qc * 2 + qz) * 4 + qy + qc * (qx - qy)],
            dst_ref=best_of.at[me_all],
            send_sem=top_sem.at[0],
            recv_sem=top_sem.at[1],
            device_id=device(qy, qx, qz, qc, (t + crossed * 2) % 4),
            device_id_type=MESH,
        )

    def send_top(i, carry):
        top_copy(i).start()
        return carry

    lax.fori_loop(1, 64, send_top, 0)

    collect(col_two, me_two, 7, 7, 8)
    col_norm[...] = HALF * jnp.log(jnp.sum(col_two[...], axis=0) * (1.0 / 65536.0))

    def row_body(i, carry):
        rows = pl.ds(pl.multiple_of(i * 32, 32), 32)
        top = None
        for step in range(8):
            mine, theirs = lines(step)
            value = cosine[step, rows, :]
            for part, line in ((value[:, :LANES], mine), (value[:, LANES:], theirs)):
                part = part - col_norm[pl.ds(line, 1), :]
                top = part if top is None else jnp.maximum(top, part)
        row_acc[rows, :] = top
        return carry

    lax.fori_loop(0, ROWS // 32, row_body, 0)
    row_max[t] = rows_of(row_acc, jnp.max)
    exchange(row_max, t, peers_row, 17, 4)

    collect(row_max, t, 3, 17, 4)
    row_ref[...] = jnp.max(row_max[...], axis=0) - row_norm[...]
    everyone = best_of.at[pl.ds(0, 63)]
    tops_in = pltpu.make_async_remote_copy(
        src_ref=everyone,
        dst_ref=everyone,
        send_sem=top_sem.at[0],
        recv_sem=top_sem.at[1],
        device_id=other_core,
        device_id_type=MESH,
    )
    tops_in.wait_recv()
    best = jnp.max(best_of[...], axis=0) - col_norm[pl.ds((c * 2 + zh) * 4 + b, 1), :]
    out = jnp.zeros((1, PIECE), jnp.float32)
    for i in range(RING):
        out = jnp.where(a == i, best[:, i * PIECE : (i + 1) * PIECE], out)
    col_ref[...] = out

    for copy in sends + pair_sends + small:
        copy.wait_send()
    tops_in.wait_send()


def local(sources, targets):
    f32, bf16 = jnp.float32, jnp.bfloat16
    dma = pltpu.SemaphoreType.DMA
    row_best, col_best = pl.pallas_call(
        kernel,
        out_shape=(
            jax.ShapeDtypeStruct((8, LANES), f32),
            jax.ShapeDtypeStruct((1, PIECE), f32),
        ),
        in_specs=[pl.BlockSpec(memory_space=pltpu.HBM)] * 2,
        out_specs=(pl.BlockSpec(memory_space=pltpu.VMEM),) * 2,
        scratch_shapes=[
            pltpu.VMEM((ROWS, DEPTH), bf16),
            pltpu.VMEM((PIECE, DEPTH), bf16),
            pltpu.VMEM((2, 2, RING, RING, PIECE, DEPTH), bf16),
            pltpu.VMEM((8, ROWS, 2 * LANES), f32),
            pltpu.VMEM((ROWS, LANES), f32),
            pltpu.VMEM((ROWS, LANES), f32),
            pltpu.VMEM((16, 8, LANES), f32),
            pltpu.VMEM((8, 16, LANES), f32),
            pltpu.VMEM((8, 16, LANES), f32),
            pltpu.VMEM((16, 1, LANES), f32),
            pltpu.VMEM((64, 1, LANES), f32),
            pltpu.VMEM((4, 8, LANES), f32),
            pltpu.VMEM((4, 8, LANES), f32),
            pltpu.VMEM((16, LANES), f32),
            pltpu.VMEM((8, LANES), f32),
            dma((2,)),
            dma((32,)),
            dma((8,)),
            dma((39,)),
            dma((20,)),
            dma((20,)),
            dma((2,)),
        ],
        compiler_params=pltpu.CompilerParams(
            collective_id=0, has_side_effects=True, vmem_limit_bytes=48 * 1024 * 1024
        ),
        cost_estimate=pl.CostEstimate(
            flops=2 * ROWS * 2048 * DEPTH, bytes_accessed=1 << 22, transcendentals=1 << 21
        ),
    )(sources, targets)
    return row_best.reshape(ROWS), col_best.reshape(PIECE)


def solution(mesh):
    in_specs = (P("src", None), P(("src", "tgt"), None))
    out_specs = (P("src"), P(("src", "tgt")))
    return jax.shard_map(local, mesh=mesh, in_specs=in_specs, out_specs=out_specs, check_vma=False)
```

```python
import functools
import math

import jax
import jax.numpy as jnp
from jax import lax
from jax.experimental import pallas as pl
from jax.experimental.pallas import tpu as pltpu
from jax.sharding import PartitionSpec as P

MESH = pl.DeviceIdType.MESH
EXP_SCALE = 20.0 * math.log2(math.e)
HALF = 0.025
RING = 4
ROWS, DEPTH, PIECE = 1024, 1024, 32
LANES = 128
ORDER = ((0, 0), (0, -1), (0, 1), (1, 0), (0, 2), (1, -1), (1, 1), (1, 2))


def plan():
    todo = []

    def send(plane, step_b, step_a, *ways):
        todo.extend(("send", plane, step_b, step_a, way) for way in ways)

    def take(plane, step_b, step_a, *ways):
        todo.append(("take", plane, step_b, step_a))
        send(plane, step_b, step_a, *ways)

    def share(*steps):
        todo.extend(("share", step) for step in steps)

    def multiply(*steps):
        todo.extend(("multiply", step) for step in steps)

    send(0, 0, 0, "z", "+a", "-a", "2a", "+b", "-b")
    todo.append(("prepare",))
    take(0, 0, -1, "+b", "-b")
    take(0, 0, 1, "+b", "-b")
    take(1, 0, 0, "+a", "-a", "2a")
    take(0, 0, 2, "+b", "-b")
    share(0)
    send(1, 0, 0, "+b", "-b", "2b")
    for d in (0, -1, 1, 2):
        take(0, -1, d, *(("+b",) if d in (0, 1) else ()))
        take(0, 1, d, *(() if d in (0, 1) else ("-b",)))
    share(1, 2)
    take(1, 0, -1, "+b", "-b")
    take(1, 0, 1, "+b", "-b")
    take(1, 0, 2, "+b", "-b")
    for d in (-1, 1, 2):
        send(1, 0, d, "2b")
    share(3)
    multiply(0, 1, 2)
    for d in (0, -1, 1, 2):
        take(0, 2, d)
    share(4)
    multiply(3)
    for d in (0, -1, 1, 2):
        take(1, -1, d)
        take(1, 1, d)
    share(5, 6)
    multiply(4)
    for d in (0, -1, 1, 2):
        take(1, 2, d)
    share(7)
    multiply(5, 6, 7)
    return todo


def unit_rows(values):
    values = values.astype(jnp.float32)
    scale = lax.rsqrt(jnp.mean(values * values, axis=1, keepdims=True) + 1e-06)
    return (values * scale * (1.0 / 32.0)).astype(jnp.bfloat16)


def kernel(
    src_ref,
    tgt_ref,
    row_ref,
    col_ref,
    unit,
    gathered,
    cosine,
    row_acc,
    row_bias,
    col_part,
    col_one,
    col_two,
    col_top,
    best_of,
    row_one,
    row_max,
    col_norm,
    row_norm,
    load_sem,
    recv_sem,
    pair_sem,
    send_sem,
    small_send,
    small_recv,
    top_sem,
):
    s = lax.axis_index("src")
    t = lax.axis_index("tgt")
    c = s % 2
    zh = (s // 2) % 2
    x = (s // 4) % 4
    y = s // 16
    a = x + c * (y - x)
    b = y + c * (x - y)

    def device(y, x, zh, c, t):
        return (((y * 4 + x) * 2 + zh) * 2 + c, t)

    def moved(da, db):
        aa, bb = (a + da + RING) % RING, (b + db + RING) % RING
        return device(bb + c * (aa - bb), aa + c * (bb - aa), zh, c, t)

    other_core = device(y, x, zh, 1 - c, t)
    other_plane = device(y, x, 1 - zh, c, (t + 2) % 4)

    load = pltpu.make_async_copy(src_ref, unit, load_sem)
    load.start()

    me_one, me_two = x * 2 + c, y * 2 + zh
    peers_one, peers_two, peers_row = [], [], []
    for i in range(1, 8):
        p = (me_one + i) % 8
        peers_one.append(device(y, p // 2, zh, p % 2, t))
        p = (me_two + i) % 8
        q = p % 2
        other = (q - zh) * (q - zh)
        peers_two.append(device(p // 2, x, q, c, (t + other * 2) % 4))
    for i in range(1, 4):
        peers_row.append(device(y, x, zh, c, (t + i) % 4))

    barrier = pltpu.get_barrier_semaphore()
    greeted = [moved(1, 0), moved(2, 0), moved(3, 0), moved(0, 1), moved(0, 2), moved(0, 3), other_core, other_plane]
    greeted += peers_row
    for peer in greeted:
        pl.semaphore_signal(barrier, inc=1, device_id=peer, device_id_type=MESH)

    def plane_of(p):
        return zh if p == 0 else 1 - zh

    def ring(v, d):
        return (v + d + RING) % RING

    gathered[c, zh, b, a] = unit_rows(tgt_ref[...])
    pl.semaphore_wait(barrier, len(greeted))

    sends = []

    def chunk_copy(p, db, da, to, send):
        pp, bb, aa = plane_of(p), ring(b, db), ring(a, da)
        slot = gathered.at[c, pp, bb, aa]
        return pltpu.make_async_remote_copy(
            src_ref=slot,
            dst_ref=slot,
            send_sem=send_sem.at[send],
            recv_sem=recv_sem.at[(pp * RING + bb) * RING + aa],
            device_id=to,
            device_id_type=MESH,
        )

    def forward(p, db, da, to):
        copy = chunk_copy(p, db, da, to, len(sends))
        copy.start()
        sends.append(copy)

    def arrived(p, db, da):
        chunk_copy(p, db, da, other_core, 0).wait_recv()

    def pair_copy(step, mine):
        p, db = ORDER[step]
        core = c if mine else 1 - c
        slot = gathered.at[core, plane_of(p), ring(b if mine else a, db)]
        return pltpu.make_async_remote_copy(
            src_ref=slot,
            dst_ref=slot,
            send_sem=send_sem.at[31 + step],
            recv_sem=pair_sem.at[step],
            device_id=other_core,
            device_id_type=MESH,
        )

    plus_a, minus_a, plus_b, minus_b = moved(1, 0), moved(-1, 0), moved(0, 1), moved(0, -1)

    ways = {
        "+a": plus_a,
        "-a": minus_a,
        "2a": moved(2, 0),
        "+b": plus_b,
        "-b": minus_b,
        "2b": moved(0, 2),
        "z": other_plane,
    }

    def share(step):
        copy = pair_copy(step, True)
        copy.start()
        pair_sends.append(copy)

    def prepare():
        load.wait()

        def body(i, carry):
            rows = pl.ds(pl.multiple_of(i * 64, 64), 64)
            unit[rows, :] = unit_rows(unit[rows, :])
            return carry

        lax.fori_loop(0, ROWS // 64, body, 0)
        row_acc[...] = jnp.zeros_like(row_acc)

    def lines(step):
        p, db = ORDER[step]
        pp = plane_of(p)
        return (c * 2 + pp) * 4 + ring(b, db), ((1 - c) * 2 + pp) * 4 + ring(a, db)

    def multiply(step):
        p, db = ORDER[step]
        pair_copy(step, False).wait_recv()
        pp = plane_of(p)
        group = jnp.concatenate(
            [
                gathered[c, pp, ring(b, db)].reshape(LANES, DEPTH),
                gathered[1 - c, pp, ring(a, db)].reshape(LANES, DEPTH),
            ],
            axis=0,
        )
        mine, theirs = lines(step)
        block = 512

        def body(i, total):
            rows = pl.ds(pl.multiple_of(i * block, block), block)
            angle = lax.dot_general(
                unit[rows, :], group, (((1,), (1,)), ((), ())), preferred_element_type=jnp.float32
            )
            cosine[step, rows, :] = angle
            share = jnp.exp2(angle * EXP_SCALE)
            row_acc[rows, :] += share[:, :LANES] + share[:, LANES:]
            return total + jnp.sum(share.reshape(block // 8, 8, 2 * LANES), axis=0)

        total = lax.fori_loop(0, ROWS // block, body, jnp.zeros((8, 2 * LANES), jnp.float32))
        col_part[mine] = total[:, :LANES]
        col_part[theirs] = total[:, LANES:]

    pair_sends = []
    for event, *at in plan():
        if event == "take":
            arrived(*at)
        elif event == "send":
            forward(*at[:3], ways[at[3]])
        elif event == "share":
            share(*at)
        elif event == "multiply":
            multiply(*at)
        else:
            prepare()

    small = []

    def exchange(buffer, me, peers, base, width):
        for i, peer in enumerate(peers):
            copy = pltpu.make_async_remote_copy(
                src_ref=buffer.at[me],
                dst_ref=buffer.at[me],
                send_sem=small_send.at[base + i],
                recv_sem=small_recv.at[base + i],
                device_id=peer,
                device_id_type=MESH,
            )
            copy.start()
            small.append(copy)

    def collect(buffer, me, count, base, width):
        for i in range(count):
            slot = buffer.at[(me + width - 1 - i) % width]
            pltpu.make_async_remote_copy(
                src_ref=slot,
                dst_ref=slot,
                send_sem=small_send.at[base + i],
                recv_sem=small_recv.at[base + i],
                device_id=other_core,
                device_id_type=MESH,
            ).wait_recv()

    def columns(reduce, source):
        return reduce(source[...], axis=1)

    def rows_of(source, reduce):
        parts = []
        for i in range(8):
            block = source[i * LANES : (i + 1) * LANES, :]
            parts.append(reduce(block.T, axis=0, keepdims=True))
        return jnp.concatenate(parts, axis=0)

    col_one[me_one] = columns(jnp.sum, col_part)
    exchange(col_one, me_one, peers_one, 0, 8)
    row_one[t] = rows_of(row_acc, jnp.sum)
    exchange(row_one, t, peers_row, 14, 4)
    collect(col_one, me_one, 7, 0, 8)
    col_two[me_two] = jnp.sum(col_one[...], axis=0)
    exchange(col_two, me_two, peers_two, 7, 8)

    collect(row_one, t, 3, 14, 4)
    row_norm[...] = HALF * jnp.log(jnp.sum(row_one[...], axis=0) * (1.0 / 8192.0))
    for i in range(8):
        line = jnp.broadcast_to(row_norm[i : i + 1, :], (LANES, LANES))
        row_bias[i * LANES : (i + 1) * LANES, :] = line.T

    def col_body(i, tops):
        rows = pl.ds(pl.multiple_of(i * 32, 32), 32)
        bias = row_bias[rows, :]
        bias = jnp.concatenate([bias, bias], axis=1)
        new = []
        for step in range(8):
            value = (cosine[step, rows, :] - bias).reshape(4, 8, 2 * LANES)
            new.append(jnp.maximum(tops[step], jnp.max(value, axis=0)))
        return tuple(new)

    start = jnp.full((8, 2 * LANES), -1e30, jnp.float32)
    tops = lax.fori_loop(0, ROWS // 32, col_body, (start,) * 8)
    for step in range(8):
        mine, theirs = lines(step)
        col_part[mine] = tops[step][:, :LANES]
        col_part[theirs] = tops[step][:, LANES:]
    col_top[...] = jnp.max(col_part[...], axis=1, keepdims=True)
    me_all = (me_two // 2 * 4 + x) * 4 + zh * 2 + c
    best_of[me_all] = col_top[(c * 2 + zh) * 4 + b]

    def top_copy(i):
        p = (me_all + i) % 64
        qc, qz, qx, qy = p % 2, (p // 2) % 2, (p // 4) % 4, p // 16
        crossed = (qz - zh) * (qz - zh)
        return pltpu.make_async_remote_copy(
            src_ref=col_top.at[(qc * 2 + qz) * 4 + qy + qc * (qx - qy)],
            dst_ref=best_of.at[me_all],
            send_sem=top_sem.at[0],
            recv_sem=top_sem.at[1],
            device_id=device(qy, qx, qz, qc, (t + crossed * 2) % 4),
            device_id_type=MESH,
        )

    def send_top(i, carry):
        top_copy(i).start()
        return carry

    lax.fori_loop(1, 64, send_top, 0)

    collect(col_two, me_two, 7, 7, 8)
    col_norm[...] = HALF * jnp.log(jnp.sum(col_two[...], axis=0) * (1.0 / 65536.0))

    def row_body(i, carry):
        rows = pl.ds(pl.multiple_of(i * 32, 32), 32)
        top = None
        for step in range(8):
            mine, theirs = lines(step)
            value = cosine[step, rows, :]
            for part, line in ((value[:, :LANES], mine), (value[:, LANES:], theirs)):
                part = part - col_norm[pl.ds(line, 1), :]
                top = part if top is None else jnp.maximum(top, part)
        row_acc[rows, :] = top
        return carry

    lax.fori_loop(0, ROWS // 32, row_body, 0)
    row_max[t] = rows_of(row_acc, jnp.max)
    exchange(row_max, t, peers_row, 17, 4)

    collect(row_max, t, 3, 17, 4)
    row_ref[...] = jnp.max(row_max[...], axis=0) - row_norm[...]
    everyone = best_of.at[pl.ds(0, 63)]
    tops_in = pltpu.make_async_remote_copy(
        src_ref=everyone,
        dst_ref=everyone,
        send_sem=top_sem.at[0],
        recv_sem=top_sem.at[1],
        device_id=other_core,
        device_id_type=MESH,
    )
    tops_in.wait_recv()
    best = jnp.max(best_of[...], axis=0) - col_norm[pl.ds((c * 2 + zh) * 4 + b, 1), :]
    out = jnp.zeros((1, PIECE), jnp.float32)
    for i in range(RING):
        out = jnp.where(a == i, best[:, i * PIECE : (i + 1) * PIECE], out)
    col_ref[...] = out

    for copy in sends + pair_sends + small:
        copy.wait_send()
    tops_in.wait_send()


def local(sources, targets):
    f32, bf16 = jnp.float32, jnp.bfloat16
    dma = pltpu.SemaphoreType.DMA
    row_best, col_best = pl.pallas_call(
        kernel,
        out_shape=(
            jax.ShapeDtypeStruct((8, LANES), f32),
            jax.ShapeDtypeStruct((1, PIECE), f32),
        ),
        in_specs=[pl.BlockSpec(memory_space=pl.ANY), pl.BlockSpec(memory_space=pltpu.VMEM)],
        out_specs=(pl.BlockSpec(memory_space=pltpu.VMEM),) * 2,
        scratch_shapes=[
            pltpu.VMEM((ROWS, DEPTH), bf16),
            pltpu.VMEM((2, 2, RING, RING, PIECE, DEPTH), bf16),
            pltpu.VMEM((8, ROWS, 2 * LANES), f32),
            pltpu.VMEM((ROWS, LANES), f32),
            pltpu.VMEM((ROWS, LANES), f32),
            pltpu.VMEM((16, 8, LANES), f32),
            pltpu.VMEM((8, 16, LANES), f32),
            pltpu.VMEM((8, 16, LANES), f32),
            pltpu.VMEM((16, 1, LANES), f32),
            pltpu.VMEM((64, 1, LANES), f32),
            pltpu.VMEM((4, 8, LANES), f32),
            pltpu.VMEM((4, 8, LANES), f32),
            pltpu.VMEM((16, LANES), f32),
            pltpu.VMEM((8, LANES), f32),
            dma,
            dma((32,)),
            dma((8,)),
            dma((39,)),
            dma((20,)),
            dma((20,)),
            dma((2,)),
        ],
        compiler_params=pltpu.CompilerParams(
            collective_id=0, has_side_effects=True, vmem_limit_bytes=53 * 1024 * 1024
        ),
        cost_estimate=pl.CostEstimate(
            flops=2 * ROWS * 2048 * DEPTH, bytes_accessed=1 << 22, transcendentals=1 << 21
        ),
    )(sources, targets)
    return row_best.reshape(ROWS), col_best.reshape(PIECE)


def solution(mesh):
    in_specs = (P("src", None), P(("src", "tgt"), None))
    out_specs = (P("src"), P(("src", "tgt")))
    return jax.shard_map(local, mesh=mesh, in_specs=in_specs, out_specs=out_specs, check_vma=False)
```

```python
import functools
import math

import jax
import jax.numpy as jnp
from jax import lax
from jax.experimental import pallas as pl
from jax.experimental.pallas import tpu as pltpu
from jax.sharding import PartitionSpec as P

MESH = pl.DeviceIdType.MESH
EXP_SCALE = 20.0 * math.log2(math.e)
HALF = 0.025
RING = 4
ROWS, DEPTH, PIECE = 1024, 1024, 32
LANES = 128
ORDER = ((0, 0), (0, -1), (0, 1), (1, 0), (0, 2), (1, -1), (1, 1), (1, 2))


def plan():
    todo = []
    halves = ((None,), (0, 1))

    def send(plane, step_b, step_a, *ways, half=None):
        todo.extend(("send", plane, step_b, step_a, half, way) for way in ways)

    def take(plane, step_b, step_a, *ways):
        for half in halves[plane]:
            todo.append(("take", plane, step_b, step_a, half))
            send(plane, step_b, step_a, *ways, half=half)

    def again(plane, step_b, step_a, *ways):
        for half in halves[plane]:
            send(plane, step_b, step_a, *ways, half=half)

    def share(*steps):
        todo.extend(("share", step) for step in steps)

    def multiply(*steps):
        todo.append(("multiply", *steps))

    send(0, 0, 0, "z", half=0)
    send(0, 0, 0, "z", half=1)
    send(0, 0, 0, "+a", "-a", "2a", "+b", "-b")
    todo.append(("prepare",))
    take(0, 0, -1, "+b", "-b")
    take(0, 0, 1, "+b", "-b")
    take(1, 0, 0, "+a", "-a", "2a")
    take(0, 0, 2, "+b", "-b")
    share(0)
    again(1, 0, 0, "+b", "-b", "2b")
    for d in (0, -1, 1, 2):
        take(0, -1, d, *(("+b",) if d in (0, 1) else ()))
        take(0, 1, d, *(() if d in (0, 1) else ("-b",)))
    share(1, 2)
    take(1, 0, -1, "+b", "-b")
    take(1, 0, 1, "+b", "-b")
    again(1, 0, -1, "2b")
    again(1, 0, 1, "2b")
    take(1, 0, 2, "+b", "-b", "2b")
    share(3)
    multiply(0, 1, 2)
    for d in (0, -1, 1, 2):
        take(0, 2, d)
    share(4)
    multiply(3)
    for d in (0, -1, 1, 2):
        take(1, -1, d)
        take(1, 1, d)
    share(5, 6)
    multiply(4)
    for d in (0, -1, 1, 2):
        take(1, 2, d)
    share(7)
    multiply(5, 6, 7)
    return todo


def unit_rows(values):
    values = values.astype(jnp.float32)
    scale = lax.rsqrt(jnp.mean(values * values, axis=1, keepdims=True) + 1e-06)
    return (values * scale * (1.0 / 32.0)).astype(jnp.bfloat16)


def kernel(
    src_ref,
    tgt_ref,
    row_ref,
    col_ref,
    unit,
    piece,
    gathered,
    cosine,
    row_acc,
    row_bias,
    col_part,
    col_one,
    col_two,
    col_top,
    best_of,
    row_one,
    row_max,
    col_norm,
    row_norm,
    load_sem,
    recv_sem,
    pair_sem,
    send_sem,
    small_send,
    small_recv,
    top_sem,
):
    s = lax.axis_index("src")
    t = lax.axis_index("tgt")
    c = s % 2
    zh = (s // 2) % 2
    x = (s // 4) % 4
    y = s // 16
    a = x + c * (y - x)
    b = y + c * (x - y)

    def device(y, x, zh, c, t):
        return (((y * 4 + x) * 2 + zh) * 2 + c, t)

    def moved(da, db):
        aa, bb = (a + da + RING) % RING, (b + db + RING) % RING
        return device(bb + c * (aa - bb), aa + c * (bb - aa), zh, c, t)

    def ring(v, d):
        return (v + d + RING) % RING

    other_core = device(y, x, zh, 1 - c, t)
    other_plane = device(y, x, 1 - zh, c, (t + 2) % 4)

    load_piece = pltpu.make_async_copy(tgt_ref, piece, load_sem.at[0])
    load_piece.start()
    load = pltpu.make_async_copy(src_ref, unit, load_sem.at[1])
    load.start()

    me_one, me_two = x * 2 + c, y * 2 + zh
    peers_one, from_one, peers_two, from_two, peers_row, from_row = [], [], [], [], [], []
    for dx, dc in ((2, 1), (2, 0), (1, 1), (3, 1), (1, 0), (3, 0), (0, 1)):
        core = (c + dc) % 2
        peers_one.append(device(y, ring(x, dx), zh, core, t))
        from_one.append(ring(x, -dx) * 2 + core)
    for dy, dz in ((2, 1), (1, 1), (3, 1), (0, 1), (2, 0), (1, 0), (3, 0)):
        plane = (zh + dz) % 2
        peers_two.append(device(ring(y, dy), x, plane, c, (t + 2 * dz) % 4))
        from_two.append(ring(y, -dy) * 2 + plane)
    for i in range(1, 4):
        peers_row.append(device(y, x, zh, c, (t + i) % 4))
        from_row.append((t + 4 - i) % 4)

    barrier = pltpu.get_barrier_semaphore()
    greeted = [moved(1, 0), moved(2, 0), moved(3, 0), moved(0, 1), moved(0, 2), moved(0, 3), other_core, other_plane]
    greeted += peers_row
    for peer in greeted:
        pl.semaphore_signal(barrier, inc=1, device_id=peer, device_id_type=MESH)

    def plane_of(p):
        return zh + p * (1 - 2 * zh)

    load_piece.wait()
    gathered[c, zh, b, a] = unit_rows(piece[...])
    pl.semaphore_wait(barrier, len(greeted))

    sends = []

    def chunk_copy(p, db, da, half, to, arrives_in, send):
        bb, aa = ring(b, db), ring(a, da)
        slot = gathered.at[c, plane_of(p), bb, aa]
        if half is not None:
            slot = slot.at[pl.ds(half * (PIECE // 2), PIECE // 2)]
        place = bb * RING + aa
        return pltpu.make_async_remote_copy(
            src_ref=slot,
            dst_ref=slot,
            send_sem=send_sem.at[send],
            recv_sem=recv_sem.at[place if arrives_in == 0 else 16 + 2 * place + half],
            device_id=to,
            device_id_type=MESH,
        )

    def forward(p, db, da, half, way):
        copy = chunk_copy(p, db, da, half, ways[way], 1 if way == "z" else p, len(sends))
        copy.start()
        sends.append(copy)

    def arrived(p, db, da, half):
        chunk_copy(p, db, da, half, other_core, p, 0).wait_recv()

    def pair_copy(step, mine, p, db):
        core = c if mine else 1 - c
        slot = gathered.at[core, plane_of(p), ring(b if mine else a, db)]
        return pltpu.make_async_remote_copy(
            src_ref=slot,
            dst_ref=slot,
            send_sem=send_sem.at[47 + step],
            recv_sem=pair_sem.at[step],
            device_id=other_core,
            device_id_type=MESH,
        )

    plus_a, minus_a, plus_b, minus_b = moved(1, 0), moved(-1, 0), moved(0, 1), moved(0, -1)

    ways = {
        "+a": plus_a,
        "-a": minus_a,
        "2a": moved(2, 0),
        "+b": plus_b,
        "-b": minus_b,
        "2b": moved(0, 2),
        "z": other_plane,
    }

    def share(step):
        copy = pair_copy(step, True, *ORDER[step])
        copy.start()
        pair_sends.append(copy)

    def prepare():
        load.wait()

        def body(i, carry):
            rows = pl.ds(pl.multiple_of(i * 64, 64), 64)
            unit[rows, :] = unit_rows(unit[rows, :])
            return carry

        lax.fori_loop(0, ROWS // 64, body, 0)
        row_acc[...] = jnp.zeros_like(row_acc)

    def lines(p, db):
        pp = plane_of(p)
        return (pp * 2 + c) * 4 + ring(b, db), (pp * 2 + 1 - c) * 4 + ring(a, db)

    def multiply_one(step, p, db):
        pair_copy(step, False, p, db).wait_recv()
        pp = plane_of(p)
        group = jnp.concatenate(
            [
                gathered[c, pp, ring(b, db)].reshape(LANES, DEPTH),
                gathered[1 - c, pp, ring(a, db)].reshape(LANES, DEPTH),
            ],
            axis=0,
        )
        mine, theirs = lines(p, db)
        angle = lax.dot_general(
            unit[...], group, (((1,), (1,)), ((), ())), preferred_element_type=jnp.float32
        )
        cosine[step] = angle
        share = jnp.exp2(angle * EXP_SCALE)
        row_acc[...] += share[:, :LANES] + share[:, LANES:]
        total = jnp.sum(share.reshape(ROWS // 8, 8, 2 * LANES), axis=0)
        col_part[mine] = total[:, :LANES]
        col_part[theirs] = total[:, LANES:]

    def multiply(*steps):
        if len(steps) == 1:
            multiply_one(steps[0], *ORDER[steps[0]])
            return

        def body(i, carry):
            p, db = ORDER[steps[0]]
            for k in range(1, len(steps)):
                p = jnp.where(i == k, ORDER[steps[k]][0], p)
                db = jnp.where(i == k, ORDER[steps[k]][1], db)
            multiply_one(steps[0] + i, p, db)
            return carry

        lax.fori_loop(0, len(steps), body, 0)

    small = []

    def exchange(slot, peers, base):
        for i, peer in enumerate(peers):
            copy = pltpu.make_async_remote_copy(
                src_ref=slot,
                dst_ref=slot,
                send_sem=small_send.at[base + i],
                recv_sem=small_recv.at[base + i],
                device_id=peer,
                device_id_type=MESH,
            )
            copy.start()
            small.append(copy)

    def collect(slots, base):
        for i, slot in enumerate(slots):
            pltpu.make_async_remote_copy(
                src_ref=slot,
                dst_ref=slot,
                send_sem=small_send.at[base + i],
                recv_sem=small_recv.at[base + i],
                device_id=other_core,
                device_id_type=MESH,
            ).wait_recv()

    def first_stage():
        col_one[me_one] = jnp.sum(col_part[...], axis=1)
        exchange(col_one.at[me_one], peers_one, 0)

    def second_stage():
        collect([col_one.at[i] for i in from_one], 0)
        col_two[me_two] = jnp.sum(col_one[...], axis=0)
        exchange(col_two.at[me_two], peers_two, 7)

    pair_sends = []
    for event, *at in plan():
        if event == "take":
            arrived(*at)
        elif event == "send":
            forward(*at)
        elif event == "share":
            share(*at)
        elif event == "multiply":
            multiply(*at)
        else:
            prepare()

    def rows_of(source, reduce):
        parts = []
        for i in range(8):
            block = source[i * LANES : (i + 1) * LANES, :]
            parts.append(reduce(block.T, axis=0, keepdims=True))
        return jnp.concatenate(parts, axis=0)

    first_stage()
    row_one[t] = rows_of(row_acc, jnp.sum)
    exchange(row_one.at[t], peers_row, 14)
    for copy in sends + pair_sends:
        copy.wait_send()
    second_stage()

    collect([row_one.at[i] for i in from_row], 14)
    row_norm[...] = HALF * jnp.log(jnp.sum(row_one[...], axis=0) * (1.0 / 8192.0))
    for i in range(8):
        line = jnp.broadcast_to(row_norm[i : i + 1, :], (LANES, LANES))
        row_bias[i * LANES : (i + 1) * LANES, :] = line.T

    def col_body(i, tops):
        rows = pl.ds(pl.multiple_of(i * 32, 32), 32)
        bias = row_bias[rows, :]
        bias = jnp.concatenate([bias, bias], axis=1)
        new = []
        for step in range(8):
            value = (cosine[step, rows, :] - bias).reshape(4, 8, 2 * LANES)
            new.append(jnp.maximum(tops[step], jnp.max(value, axis=0)))
        return tuple(new)

    start = jnp.full((8, 2 * LANES), -1e30, jnp.float32)
    tops = lax.fori_loop(0, ROWS // 32, col_body, (start,) * 8)
    for step in range(8):
        mine, theirs = lines(*ORDER[step])
        col_part[mine] = tops[step][:, :LANES]
        col_part[theirs] = tops[step][:, LANES:]
    col_top[...] = jnp.max(col_part[...], axis=1, keepdims=True)
    me_all = (me_two // 2 * 4 + x) * 4 + zh * 2 + c
    best_of[me_all] = col_top[(zh * 2 + c) * 4 + b]

    def send_top(qy, qx, qz, qc, qt):
        pltpu.make_async_remote_copy(
            src_ref=col_top.at[(qz * 2 + qc) * 4 + qy + qc * (qx - qy)],
            dst_ref=best_of.at[me_all],
            send_sem=top_sem.at[0],
            recv_sem=top_sem.at[1],
            device_id=device(qy, qx, qz, qc, qt),
            device_id_type=MESH,
        ).start()

    spots = []
    for dx in (2, 1, 3, 0):
        for dz in (1, 0):
            for dc in (1, 0):
                spots.append((ring(x, dx), (zh + dz) % 2, (c + dc) % 2, (t + 2 * dz) % 4))

    def send_tops(dy, carry):
        for spot in spots[:-1]:
            send_top(ring(y, dy), *spot)
        return carry

    lax.fori_loop(0, RING, send_tops, 0)
    for dy in (1, 2, 3):
        send_top(ring(y, dy), *spots[-1])

    collect([col_two.at[i] for i in from_two], 7)
    col_norm[...] = HALF * jnp.log(jnp.sum(col_two[...], axis=0) * (1.0 / 65536.0))

    def row_body(i, carry):
        rows = pl.ds(pl.multiple_of(i * 32, 32), 32)
        top = None
        for step in range(8):
            mine, theirs = lines(*ORDER[step])
            value = cosine[step, rows, :]
            for part, line in ((value[:, :LANES], mine), (value[:, LANES:], theirs)):
                part = part - col_norm[pl.ds(line, 1), :]
                top = part if top is None else jnp.maximum(top, part)
        row_acc[rows, :] = top
        return carry

    lax.fori_loop(0, ROWS // 32, row_body, 0)
    row_max[t] = rows_of(row_acc, jnp.max)
    exchange(row_max.at[t], peers_row, 17)

    for copy in small:
        copy.wait_send()
    collect([row_max.at[i] for i in from_row], 17)
    row_ref[...] = jnp.max(row_max[...], axis=0) - row_norm[...]
    everyone = best_of.at[pl.ds(0, 63)]
    tops_in = pltpu.make_async_remote_copy(
        src_ref=everyone,
        dst_ref=everyone,
        send_sem=top_sem.at[0],
        recv_sem=top_sem.at[1],
        device_id=other_core,
        device_id_type=MESH,
    )
    tops_in.wait_recv()
    best = jnp.max(best_of[...], axis=0) - col_norm[pl.ds((zh * 2 + c) * 4 + b, 1), :]
    out = jnp.zeros((1, PIECE), jnp.float32)
    for i in range(RING):
        out = jnp.where(a == i, best[:, i * PIECE : (i + 1) * PIECE], out)
    col_ref[...] = out

    tops_in.wait_send()


def local(sources, targets):
    f32, bf16 = jnp.float32, jnp.bfloat16
    dma = pltpu.SemaphoreType.DMA
    row_best, col_best = pl.pallas_call(
        kernel,
        out_shape=(
            jax.ShapeDtypeStruct((8, LANES), f32),
            jax.ShapeDtypeStruct((1, PIECE), f32),
        ),
        in_specs=[pl.BlockSpec(memory_space=pl.ANY)] * 2,
        out_specs=(pl.BlockSpec(memory_space=pltpu.VMEM),) * 2,
        scratch_shapes=[
            pltpu.VMEM((ROWS, DEPTH), bf16),
            pltpu.VMEM((PIECE, DEPTH), bf16),
            pltpu.VMEM((2, 2, RING, RING, PIECE, DEPTH), bf16),
            pltpu.VMEM((8, ROWS, 2 * LANES), f32),
            pltpu.VMEM((ROWS, LANES), f32),
            pltpu.VMEM((ROWS, LANES), f32),
            pltpu.VMEM((16, 8, LANES), f32),
            pltpu.VMEM((8, 16, LANES), f32),
            pltpu.VMEM((8, 16, LANES), f32),
            pltpu.VMEM((16, 1, LANES), f32),
            pltpu.VMEM((64, 1, LANES), f32),
            pltpu.VMEM((4, 8, LANES), f32),
            pltpu.VMEM((4, 8, LANES), f32),
            pltpu.VMEM((16, LANES), f32),
            pltpu.VMEM((8, LANES), f32),
            dma((2,)),
            dma((48,)),
            dma((8,)),
            dma((55,)),
            dma((20,)),
            dma((20,)),
            dma((2,)),
        ],
        compiler_params=pltpu.CompilerParams(
            collective_id=0, has_side_effects=True, vmem_limit_bytes=55193 * 1024
        ),
        cost_estimate=pl.CostEstimate(
            flops=2 * ROWS * 2048 * DEPTH, bytes_accessed=1 << 22, transcendentals=1 << 21
        ),
    )(sources, targets)
    return row_best.reshape(ROWS), col_best.reshape(PIECE)


def solution(mesh):
    in_specs = (P("src", None), P(("src", "tgt"), None))
    out_specs = (P("src"), P(("src", "tgt")))
    return jax.shard_map(local, mesh=mesh, in_specs=in_specs, out_specs=out_specs, check_vma=False)
```

```python
import functools
import math

import jax
import jax.numpy as jnp
from jax import lax
from jax.experimental import pallas as pl
from jax.experimental.pallas import tpu as pltpu
from jax.sharding import PartitionSpec as P

MESH = pl.DeviceIdType.MESH
EXP_SCALE = 20.0 * math.log2(math.e)
HALF = 0.025
RING = 4
ROWS, DEPTH, PIECE = 1024, 1024, 32
LANES = 128
ORDER = ((0, 0), (0, -1), (0, 1), (1, 0), (0, 2), (1, -1), (1, 1), (1, 2))


def plan():
    todo = []
    halves = ((None,), (0, 1))

    def send(plane, step_b, step_a, *ways, half=None):
        todo.extend(("send", plane, step_b, step_a, half, way) for way in ways)

    def take(plane, step_b, step_a, *ways):
        for half in halves[plane]:
            todo.append(("take", plane, step_b, step_a, half))
            send(plane, step_b, step_a, *ways, half=half)

    def again(plane, step_b, step_a, *ways):
        for half in halves[plane]:
            send(plane, step_b, step_a, *ways, half=half)

    def share(*steps):
        todo.extend(("share", step) for step in steps)

    def multiply(*steps):
        todo.append(("multiply", *steps))

    send(0, 0, 0, "z", half=0)
    send(0, 0, 0, "z", half=1)
    send(0, 0, 0, "+a", "-a", "2a", "+b", "-b")
    todo.append(("prepare",))
    take(0, 0, -1, "+b", "-b")
    take(0, 0, 1, "+b", "-b")
    take(1, 0, 0, "+a", "-a", "2a")
    take(0, 0, 2, "+b", "-b")
    share(0)
    again(1, 0, 0, "+b", "-b", "2b")
    for d in (0, -1, 1, 2):
        take(0, -1, d, *(("+b",) if d in (0, 1) else ()))
        take(0, 1, d, *(() if d in (0, 1) else ("-b",)))
    share(1, 2)
    take(1, 0, -1, "+b", "-b")
    take(1, 0, 1, "+b", "-b")
    take(1, 0, 2, "+b", "-b", "2b")
    share(3)
    multiply(0, 1, 2)
    take(1, -1, -1, "+b")
    take(1, 1, 1, "-b")
    for d in (0, -1, 1, 2):
        take(0, 2, d)
    share(4)
    multiply(3)
    for d in (0, -1, 1, 2):
        if d != -1:
            take(1, -1, d)
        if d != 1:
            take(1, 1, d)
    share(5, 6)
    multiply(4)
    for d in (0, -1, 1, 2):
        take(1, 2, d)
    share(7)
    multiply(5, 6, 7)
    return todo


def unit_rows(values):
    values = values.astype(jnp.float32)
    scale = lax.rsqrt(jnp.mean(values * values, axis=1, keepdims=True) + 1e-06)
    return (values * scale * (1.0 / 32.0)).astype(jnp.bfloat16)


def kernel(
    src_ref,
    tgt_ref,
    row_ref,
    col_ref,
    unit,
    piece,
    gathered,
    cosine,
    row_acc,
    row_bias,
    col_part,
    col_one,
    col_two,
    col_top,
    best_of,
    row_one,
    row_max,
    col_norm,
    row_norm,
    load_sem,
    recv_sem,
    pair_sem,
    send_sem,
    small_send,
    small_recv,
    top_sem,
):
    s = lax.axis_index("src")
    t = lax.axis_index("tgt")
    c = s % 2
    zh = (s // 2) % 2
    x = (s // 4) % 4
    y = s // 16
    a = x + c * (y - x)
    b = y + c * (x - y)

    def device(y, x, zh, c, t):
        return (((y * 4 + x) * 2 + zh) * 2 + c, t)

    def moved(da, db):
        aa, bb = (a + da + RING) % RING, (b + db + RING) % RING
        return device(bb + c * (aa - bb), aa + c * (bb - aa), zh, c, t)

    def ring(v, d):
        return (v + d + RING) % RING

    other_core = device(y, x, zh, 1 - c, t)
    other_plane = device(y, x, 1 - zh, c, (t + 2) % 4)

    load_piece = pltpu.make_async_copy(tgt_ref, piece, load_sem.at[0])
    load_piece.start()
    load = pltpu.make_async_copy(src_ref, unit, load_sem.at[1])
    load.start()

    me_one, me_two = x * 2 + c, y * 2 + zh
    peers_one, from_one, peers_two, from_two, peers_row, from_row = [], [], [], [], [], []
    for dx, dc in ((2, 1), (2, 0), (1, 1), (3, 1), (1, 0), (3, 0), (0, 1)):
        core = (c + dc) % 2
        peers_one.append(device(y, ring(x, dx), zh, core, t))
        from_one.append(ring(x, -dx) * 2 + core)
    for dy, dz in ((2, 1), (1, 1), (3, 1), (0, 1), (2, 0), (1, 0), (3, 0)):
        plane = (zh + dz) % 2
        peers_two.append(device(ring(y, dy), x, plane, c, (t + 2 * dz) % 4))
        from_two.append(ring(y, -dy) * 2 + plane)
    for i in range(1, 4):
        peers_row.append(device(y, x, zh, c, (t + i) % 4))
        from_row.append((t + 4 - i) % 4)

    barrier = pltpu.get_barrier_semaphore()
    greeted = [moved(1, 0), moved(2, 0), moved(3, 0), moved(0, 1), moved(0, 2), moved(0, 3), other_core, other_plane]
    greeted += peers_row
    for peer in greeted:
        pl.semaphore_signal(barrier, inc=1, device_id=peer, device_id_type=MESH)

    def plane_of(p):
        return zh + p * (1 - 2 * zh)

    load_piece.wait()
    gathered[c, zh, b, a] = unit_rows(piece[...])
    pl.semaphore_wait(barrier, len(greeted))

    sends = []

    def chunk_copy(p, db, da, half, to, arrives_in, send):
        bb, aa = ring(b, db), ring(a, da)
        slot = gathered.at[c, plane_of(p), bb, aa]
        if half is not None:
            slot = slot.at[pl.ds(half * (PIECE // 2), PIECE // 2)]
        place = bb * RING + aa
        return pltpu.make_async_remote_copy(
            src_ref=slot,
            dst_ref=slot,
            send_sem=send_sem.at[send],
            recv_sem=recv_sem.at[place if arrives_in == 0 else 16 + 2 * place + half],
            device_id=to,
            device_id_type=MESH,
        )

    def forward(p, db, da, half, way):
        copy = chunk_copy(p, db, da, half, ways[way], 1 if way == "z" else p, len(sends))
        copy.start()
        sends.append(copy)

    def arrived(p, db, da, half):
        chunk_copy(p, db, da, half, other_core, p, 0).wait_recv()

    def pair_copy(step, mine, p, db):
        core = c if mine else 1 - c
        slot = gathered.at[core, plane_of(p), ring(b if mine else a, db)]
        return pltpu.make_async_remote_copy(
            src_ref=slot,
            dst_ref=slot,
            send_sem=send_sem.at[47 + step],
            recv_sem=pair_sem.at[step],
            device_id=other_core,
            device_id_type=MESH,
        )

    plus_a, minus_a, plus_b, minus_b = moved(1, 0), moved(-1, 0), moved(0, 1), moved(0, -1)

    ways = {
        "+a": plus_a,
        "-a": minus_a,
        "2a": moved(2, 0),
        "+b": plus_b,
        "-b": minus_b,
        "2b": moved(0, 2),
        "z": other_plane,
    }

    def share(step):
        copy = pair_copy(step, True, *ORDER[step])
        copy.start()
        pair_sends.append(copy)

    def prepare():
        load.wait()

        def body(i, carry):
            rows = pl.ds(pl.multiple_of(i * 64, 64), 64)
            unit[rows, :] = unit_rows(unit[rows, :])
            return carry

        lax.fori_loop(0, ROWS // 64, body, 0)
        row_acc[...] = jnp.zeros_like(row_acc)

    def lines(p, db):
        pp = plane_of(p)
        return (pp * 2 + c) * 4 + ring(b, db), (pp * 2 + 1 - c) * 4 + ring(a, db)

    def multiply_one(step, p, db):
        pair_copy(step, False, p, db).wait_recv()
        pp = plane_of(p)
        group = jnp.concatenate(
            [
                gathered[c, pp, ring(b, db)].reshape(LANES, DEPTH),
                gathered[1 - c, pp, ring(a, db)].reshape(LANES, DEPTH),
            ],
            axis=0,
        )
        mine, theirs = lines(p, db)
        angle = lax.dot_general(
            unit[...], group, (((1,), (1,)), ((), ())), preferred_element_type=jnp.float32
        )
        cosine[step] = angle
        share = jnp.exp2(angle * EXP_SCALE)
        row_acc[...] += share[:, :LANES] + share[:, LANES:]
        total = jnp.sum(share.reshape(ROWS // 8, 8, 2 * LANES), axis=0)
        col_part[mine] = total[:, :LANES]
        col_part[theirs] = total[:, LANES:]

    def multiply(*steps):
        if len(steps) == 1:
            multiply_one(steps[0], *ORDER[steps[0]])
            return

        def body(i, carry):
            p, db = ORDER[steps[0]]
            for k in range(1, len(steps)):
                p = jnp.where(i == k, ORDER[steps[k]][0], p)
                db = jnp.where(i == k, ORDER[steps[k]][1], db)
            multiply_one(steps[0] + i, p, db)
            return carry

        lax.fori_loop(0, len(steps), body, 0)

    small = []

    def exchange(slot, peers, base):
        for i, peer in enumerate(peers):
            copy = pltpu.make_async_remote_copy(
                src_ref=slot,
                dst_ref=slot,
                send_sem=small_send.at[base + i],
                recv_sem=small_recv.at[base + i],
                device_id=peer,
                device_id_type=MESH,
            )
            copy.start()
            small.append(copy)

    def collect(slots, base):
        for i, slot in enumerate(slots):
            pltpu.make_async_remote_copy(
                src_ref=slot,
                dst_ref=slot,
                send_sem=small_send.at[base + i],
                recv_sem=small_recv.at[base + i],
                device_id=other_core,
                device_id_type=MESH,
            ).wait_recv()

    def first_stage():
        col_one[me_one] = jnp.sum(col_part[...], axis=1)
        exchange(col_one.at[me_one], peers_one, 0)

    def second_stage():
        collect([col_one.at[i] for i in from_one], 0)
        col_two[me_two] = jnp.sum(col_one[...], axis=0)
        exchange(col_two.at[me_two], peers_two, 7)

    pair_sends = []
    for event, *at in plan():
        if event == "take":
            arrived(*at)
        elif event == "send":
            forward(*at)
        elif event == "share":
            share(*at)
        elif event == "multiply":
            multiply(*at)
        else:
            prepare()

    def rows_of(source, reduce):
        parts = []
        for i in range(8):
            block = source[i * LANES : (i + 1) * LANES, :]
            parts.append(reduce(block.T, axis=0, keepdims=True))
        return jnp.concatenate(parts, axis=0)

    first_stage()
    row_one[t] = rows_of(row_acc, jnp.sum)
    exchange(row_one.at[t], peers_row, 14)
    for copy in sends + pair_sends:
        copy.wait_send()
    second_stage()

    collect([row_one.at[i] for i in from_row], 14)
    row_norm[...] = HALF * jnp.log(jnp.sum(row_one[...], axis=0) * (1.0 / 8192.0))
    for i in range(8):
        line = jnp.broadcast_to(row_norm[i : i + 1, :], (LANES, LANES))
        row_bias[i * LANES : (i + 1) * LANES, :] = line.T

    def col_body(i, tops):
        rows = pl.ds(pl.multiple_of(i * 32, 32), 32)
        bias = row_bias[rows, :]
        bias = jnp.concatenate([bias, bias], axis=1)
        new = []
        for step in range(8):
            value = (cosine[step, rows, :] - bias).reshape(4, 8, 2 * LANES)
            new.append(jnp.maximum(tops[step], jnp.max(value, axis=0)))
        return tuple(new)

    start = jnp.full((8, 2 * LANES), -1e30, jnp.float32)
    tops = lax.fori_loop(0, ROWS // 32, col_body, (start,) * 8)
    for step in range(8):
        mine, theirs = lines(*ORDER[step])
        col_part[mine] = tops[step][:, :LANES]
        col_part[theirs] = tops[step][:, LANES:]
    col_top[...] = jnp.max(col_part[...], axis=1, keepdims=True)
    me_all = (me_two // 2 * 4 + x) * 4 + zh * 2 + c
    best_of[me_all] = col_top[(zh * 2 + c) * 4 + b]

    def send_top(qy, qx, qz, qc, qt):
        pltpu.make_async_remote_copy(
            src_ref=col_top.at[(qz * 2 + qc) * 4 + qy + qc * (qx - qy)],
            dst_ref=best_of.at[me_all],
            send_sem=top_sem.at[0],
            recv_sem=top_sem.at[1],
            device_id=device(qy, qx, qz, qc, qt),
            device_id_type=MESH,
        ).start()

    spots = []
    for dx in (2, 1, 3, 0):
        for dz in (1, 0):
            for dc in (1, 0):
                spots.append((ring(x, dx), (zh + dz) % 2, (c + dc) % 2, (t + 2 * dz) % 4))

    def send_tops(dy, carry):
        for spot in spots[:-1]:
            send_top(ring(y, dy), *spot)
        return carry

    lax.fori_loop(0, RING, send_tops, 0)
    for dy in (1, 2, 3):
        send_top(ring(y, dy), *spots[-1])

    collect([col_two.at[i] for i in from_two], 7)
    col_norm[...] = HALF * jnp.log(jnp.sum(col_two[...], axis=0) * (1.0 / 65536.0))

    def row_body(i, carry):
        rows = pl.ds(pl.multiple_of(i * 32, 32), 32)
        top = None
        for step in range(8):
            mine, theirs = lines(*ORDER[step])
            value = cosine[step, rows, :]
            for part, line in ((value[:, :LANES], mine), (value[:, LANES:], theirs)):
                part = part - col_norm[pl.ds(line, 1), :]
                top = part if top is None else jnp.maximum(top, part)
        row_acc[rows, :] = top
        return carry

    lax.fori_loop(0, ROWS // 32, row_body, 0)
    row_max[t] = rows_of(row_acc, jnp.max)
    exchange(row_max.at[t], peers_row, 17)

    for copy in small:
        copy.wait_send()
    collect([row_max.at[i] for i in from_row], 17)
    row_ref[...] = jnp.max(row_max[...], axis=0) - row_norm[...]
    everyone = best_of.at[pl.ds(0, 63)]
    tops_in = pltpu.make_async_remote_copy(
        src_ref=everyone,
        dst_ref=everyone,
        send_sem=top_sem.at[0],
        recv_sem=top_sem.at[1],
        device_id=other_core,
        device_id_type=MESH,
    )
    tops_in.wait_recv()
    best = jnp.max(best_of[...], axis=0) - col_norm[pl.ds((zh * 2 + c) * 4 + b, 1), :]
    out = jnp.zeros((1, PIECE), jnp.float32)
    for i in range(RING):
        out = jnp.where(a == i, best[:, i * PIECE : (i + 1) * PIECE], out)
    col_ref[...] = out

    tops_in.wait_send()


def local(sources, targets):
    f32, bf16 = jnp.float32, jnp.bfloat16
    dma = pltpu.SemaphoreType.DMA
    row_best, col_best = pl.pallas_call(
        kernel,
        out_shape=(
            jax.ShapeDtypeStruct((8, LANES), f32),
            jax.ShapeDtypeStruct((1, PIECE), f32),
        ),
        in_specs=[pl.BlockSpec(memory_space=pl.ANY)] * 2,
        out_specs=(pl.BlockSpec(memory_space=pltpu.VMEM),) * 2,
        scratch_shapes=[
            pltpu.VMEM((ROWS, DEPTH), bf16),
            pltpu.VMEM((PIECE, DEPTH), bf16),
            pltpu.VMEM((2, 2, RING, RING, PIECE, DEPTH), bf16),
            pltpu.VMEM((8, ROWS, 2 * LANES), f32),
            pltpu.VMEM((ROWS, LANES), f32),
            pltpu.VMEM((ROWS, LANES), f32),
            pltpu.VMEM((16, 8, LANES), f32),
            pltpu.VMEM((8, 16, LANES), f32),
            pltpu.VMEM((8, 16, LANES), f32),
            pltpu.VMEM((16, 1, LANES), f32),
            pltpu.VMEM((64, 1, LANES), f32),
            pltpu.VMEM((4, 8, LANES), f32),
            pltpu.VMEM((4, 8, LANES), f32),
            pltpu.VMEM((16, LANES), f32),
            pltpu.VMEM((8, LANES), f32),
            dma((2,)),
            dma((48,)),
            dma((8,)),
            dma((55,)),
            dma((20,)),
            dma((20,)),
            dma((2,)),
        ],
        compiler_params=pltpu.CompilerParams(
            collective_id=0, has_side_effects=True, vmem_limit_bytes=55193 * 1024
        ),
        cost_estimate=pl.CostEstimate(
            flops=2 * ROWS * 2048 * DEPTH, bytes_accessed=1 << 22, transcendentals=1 << 21
        ),
    )(sources, targets)
    return row_best.reshape(ROWS), col_best.reshape(PIECE)


def solution(mesh):
    in_specs = (P("src", None), P(("src", "tgt"), None))
    out_specs = (P("src"), P(("src", "tgt")))
    return jax.shard_map(local, mesh=mesh, in_specs=in_specs, out_specs=out_specs, check_vma=False)
```

```python
import functools
import math

import jax
import jax.numpy as jnp
from jax import lax
from jax.experimental import pallas as pl
from jax.experimental.pallas import tpu as pltpu
from jax.sharding import PartitionSpec as P

MESH = pl.DeviceIdType.MESH
EXP_SCALE = 20.0 * math.log2(math.e)
HALF = 0.025
RING = 4
ROWS, DEPTH, PIECE = 1024, 1024, 32
LANES = 128
ORDER = ((0, 0), (0, -1), (0, 1), (1, 0), (0, 2), (1, -1), (1, 1), (1, 2))


def plan():
    todo = []
    halves = ((None,), (0, 1))

    def send(plane, step_b, step_a, *ways, half=None):
        todo.extend(("send", plane, step_b, step_a, half, way) for way in ways)

    def take(plane, step_b, step_a, *ways):
        for half in halves[plane]:
            todo.append(("take", plane, step_b, step_a, half))
            send(plane, step_b, step_a, *ways, half=half)

    def again(plane, step_b, step_a, *ways):
        for half in halves[plane]:
            send(plane, step_b, step_a, *ways, half=half)

    def share(*steps):
        todo.extend(("share", step) for step in steps)

    def multiply(*steps):
        todo.append(("multiply", *steps))

    send(0, 0, 0, "z", half=0)
    send(0, 0, 0, "z", half=1)
    send(0, 0, 0, "+a", "-a", "2a", "+b", "-b")
    todo.append(("prepare",))
    take(0, 0, -1, "+b", "-b")
    take(0, 0, 1, "+b", "-b")
    take(1, 0, 0, "+a", "-a", "2a")
    take(0, 0, 2, "+b", "-b")
    share(0)
    again(1, 0, 0, "+b", "-b", "2b")
    for d in (0, -1, 1, 2):
        take(0, -1, d, *(("+b",) if d in (0, 1) else ()))
        take(0, 1, d, *(() if d in (0, 1) else ("-b",)))
    share(1, 2)
    take(1, 0, -1, "+b", "-b")
    take(1, 0, 1, "+b", "-b")
    take(1, 0, 2, "+b", "-b", "2b")
    share(3)
    multiply(0, 1, 2)
    take(1, -1, -1, "+b")
    take(1, 1, 1, "-b")
    for d in (0, -1, 1, 2):
        take(0, 2, d)
    share(4)
    multiply(3)
    for d in (0, -1, 1, 2):
        if d != -1:
            take(1, -1, d)
        if d != 1:
            take(1, 1, d)
    share(5, 6)
    multiply(4)
    for d in (0, -1, 1, 2):
        take(1, 2, d)
    share(7)
    multiply(5, 6, 7)
    return todo


def unit_rows(values):
    values = values.astype(jnp.float32)
    scale = lax.rsqrt(jnp.mean(values * values, axis=1, keepdims=True) + 1e-06)
    return (values * (scale * (1.0 / 32.0))).astype(jnp.bfloat16)


def kernel(
    src_ref,
    tgt_ref,
    row_ref,
    col_ref,
    unit,
    piece,
    gathered,
    cosine,
    row_acc,
    row_bias,
    col_part,
    col_one,
    col_two,
    col_top,
    best_of,
    row_one,
    row_max,
    col_norm,
    row_norm,
    load_sem,
    recv_sem,
    pair_sem,
    send_sem,
    small_send,
    small_recv,
    top_sem,
):
    s = lax.axis_index("src")
    t = lax.axis_index("tgt")
    c = s % 2
    zh = (s // 2) % 2
    x = (s // 4) % 4
    y = s // 16
    a = x + c * (y - x)
    b = y + c * (x - y)

    def device(y, x, zh, c, t):
        return (((y * 4 + x) * 2 + zh) * 2 + c, t)

    def moved(da, db):
        aa, bb = (a + da + RING) % RING, (b + db + RING) % RING
        return device(bb + c * (aa - bb), aa + c * (bb - aa), zh, c, t)

    def ring(v, d):
        return (v + d + RING) % RING

    other_core = device(y, x, zh, 1 - c, t)
    other_plane = device(y, x, 1 - zh, c, (t + 2) % 4)

    load_piece = pltpu.make_async_copy(tgt_ref, piece, load_sem.at[0])
    load_piece.start()
    load = pltpu.make_async_copy(src_ref, unit, load_sem.at[1])
    load.start()

    me_one, me_two = x * 2 + c, y * 2 + zh
    peers_one, from_one, peers_two, from_two, peers_row, from_row = [], [], [], [], [], []
    for dx, dc in ((2, 1), (2, 0), (1, 1), (3, 1), (1, 0), (3, 0), (0, 1)):
        core = (c + dc) % 2
        peers_one.append(device(y, ring(x, dx), zh, core, t))
        from_one.append(ring(x, -dx) * 2 + core)
    for dy, dz in ((2, 1), (1, 1), (3, 1), (0, 1), (2, 0), (1, 0), (3, 0)):
        plane = (zh + dz) % 2
        peers_two.append(device(ring(y, dy), x, plane, c, (t + 2 * dz) % 4))
        from_two.append(ring(y, -dy) * 2 + plane)
    for i in range(1, 4):
        peers_row.append(device(y, x, zh, c, (t + i) % 4))
        from_row.append((t + 4 - i) % 4)

    barrier = pltpu.get_barrier_semaphore()
    greeted = [moved(1, 0), moved(2, 0), moved(3, 0), moved(0, 1), moved(0, 2), moved(0, 3), other_core, other_plane]
    greeted += peers_row
    for peer in greeted:
        pl.semaphore_signal(barrier, inc=1, device_id=peer, device_id_type=MESH)

    def plane_of(p):
        return zh + p * (1 - 2 * zh)

    load_piece.wait()
    gathered[c, zh, b, a] = unit_rows(piece[...])
    pl.semaphore_wait(barrier, len(greeted))

    sends = []

    def chunk_copy(p, db, da, half, to, arrives_in, send):
        bb, aa = ring(b, db), ring(a, da)
        slot = gathered.at[c, plane_of(p), bb, aa]
        if half is not None:
            slot = slot.at[pl.ds(half * (PIECE // 2), PIECE // 2)]
        place = bb * RING + aa
        return pltpu.make_async_remote_copy(
            src_ref=slot,
            dst_ref=slot,
            send_sem=send_sem.at[send],
            recv_sem=recv_sem.at[place if arrives_in == 0 else 16 + 2 * place + half],
            device_id=to,
            device_id_type=MESH,
        )

    def forward(p, db, da, half, way):
        copy = chunk_copy(p, db, da, half, ways[way], 1 if way == "z" else p, len(sends))
        copy.start()
        sends.append(copy)

    def arrived(p, db, da, half):
        chunk_copy(p, db, da, half, other_core, p, 0).wait_recv()

    def pair_copy(step, mine, p, db):
        core = c if mine else 1 - c
        slot = gathered.at[core, plane_of(p), ring(b if mine else a, db)]
        return pltpu.make_async_remote_copy(
            src_ref=slot,
            dst_ref=slot,
            send_sem=send_sem.at[47 + step],
            recv_sem=pair_sem.at[step],
            device_id=other_core,
            device_id_type=MESH,
        )

    plus_a, minus_a, plus_b, minus_b = moved(1, 0), moved(-1, 0), moved(0, 1), moved(0, -1)

    ways = {
        "+a": plus_a,
        "-a": minus_a,
        "2a": moved(2, 0),
        "+b": plus_b,
        "-b": minus_b,
        "2b": moved(0, 2),
        "z": other_plane,
    }

    def share(step):
        copy = pair_copy(step, True, *ORDER[step])
        copy.start()
        pair_sends.append(copy)

    def prepare():
        load.wait()

        def body(i, carry):
            rows = pl.ds(pl.multiple_of(i * 64, 64), 64)
            unit[rows, :] = unit_rows(unit[rows, :])
            return carry

        lax.fori_loop(0, ROWS // 64, body, 0)
        row_acc[...] = jnp.zeros_like(row_acc)

    def lines(p, db):
        pp = plane_of(p)
        return (pp * 2 + c) * 4 + ring(b, db), (pp * 2 + 1 - c) * 4 + ring(a, db)

    def multiply_one(step, p, db):
        pair_copy(step, False, p, db).wait_recv()
        pp = plane_of(p)
        group = jnp.concatenate(
            [
                gathered[c, pp, ring(b, db)].reshape(LANES, DEPTH),
                gathered[1 - c, pp, ring(a, db)].reshape(LANES, DEPTH),
            ],
            axis=0,
        )
        mine, theirs = lines(p, db)
        angle = lax.dot_general(
            unit[...], group, (((1,), (1,)), ((), ())), preferred_element_type=jnp.float32
        )
        cosine[step] = angle
        share = jnp.exp2(angle * EXP_SCALE)
        row_acc[...] += share[:, :LANES] + share[:, LANES:]
        total = jnp.sum(share.reshape(ROWS // 8, 8, 2 * LANES), axis=0)
        col_part[mine] = total[:, :LANES]
        col_part[theirs] = total[:, LANES:]

    def multiply(*steps):
        if len(steps) == 1:
            multiply_one(steps[0], *ORDER[steps[0]])
            return

        def body(i, carry):
            p, db = ORDER[steps[0]]
            for k in range(1, len(steps)):
                p = jnp.where(i == k, ORDER[steps[k]][0], p)
                db = jnp.where(i == k, ORDER[steps[k]][1], db)
            multiply_one(steps[0] + i, p, db)
            return carry

        lax.fori_loop(0, len(steps), body, 0)

    small = []

    def exchange(slot, peers, base):
        for i, peer in enumerate(peers):
            copy = pltpu.make_async_remote_copy(
                src_ref=slot,
                dst_ref=slot,
                send_sem=small_send.at[base + i],
                recv_sem=small_recv.at[base + i],
                device_id=peer,
                device_id_type=MESH,
            )
            copy.start()
            small.append(copy)

    def collect(slots, base):
        for i, slot in enumerate(slots):
            pltpu.make_async_remote_copy(
                src_ref=slot,
                dst_ref=slot,
                send_sem=small_send.at[base + i],
                recv_sem=small_recv.at[base + i],
                device_id=other_core,
                device_id_type=MESH,
            ).wait_recv()

    def first_stage():
        col_one[me_one] = jnp.sum(col_part[...], axis=1)
        exchange(col_one.at[me_one], peers_one, 0)

    def second_stage():
        collect([col_one.at[i] for i in from_one], 0)
        col_two[me_two] = jnp.sum(col_one[...], axis=0)
        exchange(col_two.at[me_two], peers_two, 7)

    pair_sends = []
    for event, *at in plan():
        if event == "take":
            arrived(*at)
        elif event == "send":
            forward(*at)
        elif event == "share":
            share(*at)
        elif event == "multiply":
            multiply(*at)
        else:
            prepare()

    def rows_of(source, reduce):
        parts = []
        for i in range(8):
            block = source[i * LANES : (i + 1) * LANES, :]
            parts.append(reduce(block.T, axis=0, keepdims=True))
        return jnp.concatenate(parts, axis=0)

    first_stage()
    row_one[t] = rows_of(row_acc, jnp.sum)
    exchange(row_one.at[t], peers_row, 14)
    for copy in sends + pair_sends:
        copy.wait_send()
    second_stage()

    collect([row_one.at[i] for i in from_row], 14)
    row_norm[...] = HALF * jnp.log(jnp.sum(row_one[...], axis=0) * (1.0 / 8192.0))
    for i in range(8):
        line = jnp.broadcast_to(row_norm[i : i + 1, :], (LANES, LANES))
        row_bias[i * LANES : (i + 1) * LANES, :] = line.T

    def col_body(i, tops):
        rows = pl.ds(pl.multiple_of(i * 32, 32), 32)
        bias = row_bias[rows, :]
        bias = jnp.concatenate([bias, bias], axis=1)
        new = []
        for step in range(8):
            value = (cosine[step, rows, :] - bias).reshape(4, 8, 2 * LANES)
            new.append(jnp.maximum(tops[step], jnp.max(value, axis=0)))
        return tuple(new)

    start = jnp.full((8, 2 * LANES), -1e30, jnp.float32)
    tops = lax.fori_loop(0, ROWS // 32, col_body, (start,) * 8)
    for step in range(8):
        mine, theirs = lines(*ORDER[step])
        col_part[mine] = tops[step][:, :LANES]
        col_part[theirs] = tops[step][:, LANES:]
    col_top[...] = jnp.max(col_part[...], axis=1, keepdims=True)
    me_all = (me_two // 2 * 4 + x) * 4 + zh * 2 + c
    best_of[me_all] = col_top[(zh * 2 + c) * 4 + b]

    def send_top(qy, qx, qz, qc, qt):
        pltpu.make_async_remote_copy(
            src_ref=col_top.at[(qz * 2 + qc) * 4 + qy + qc * (qx - qy)],
            dst_ref=best_of.at[me_all],
            send_sem=top_sem.at[0],
            recv_sem=top_sem.at[1],
            device_id=device(qy, qx, qz, qc, qt),
            device_id_type=MESH,
        ).start()

    spots = []
    for dx in (2, 1, 3, 0):
        for dz in (1, 0):
            for dc in (1, 0):
                spots.append((ring(x, dx), (zh + dz) % 2, (c + dc) % 2, (t + 2 * dz) % 4))

    def send_tops(dy, carry):
        for spot in spots[:-1]:
            send_top(ring(y, dy), *spot)
        return carry

    lax.fori_loop(0, RING, send_tops, 0)
    for dy in (1, 2, 3):
        send_top(ring(y, dy), *spots[-1])

    collect([col_two.at[i] for i in from_two], 7)
    col_norm[...] = HALF * jnp.log(jnp.sum(col_two[...], axis=0) * (1.0 / 65536.0))

    norms = []
    for step in range(8):
        for line in lines(*ORDER[step]):
            norms.append(jnp.broadcast_to(col_norm[pl.ds(line, 1), :], (8, LANES)))

    def row_body(i, carry):
        rows = pl.ds(pl.multiple_of(i * 32, 32), 32)
        top = None
        for step in range(8):
            value = cosine[step, rows, :]
            for k in range(2):
                part = value[:, k * LANES : (k + 1) * LANES].reshape(4, 8, LANES) - norms[2 * step + k]
                top = part if top is None else jnp.maximum(top, part)
        row_acc[rows, :] = top.reshape(32, LANES)
        return carry

    lax.fori_loop(0, ROWS // 32, row_body, 0)
    row_max[t] = rows_of(row_acc, jnp.max)
    exchange(row_max.at[t], peers_row, 17)

    for copy in small:
        copy.wait_send()
    collect([row_max.at[i] for i in from_row], 17)
    row_ref[...] = jnp.max(row_max[...], axis=0) - row_norm[...]
    everyone = best_of.at[pl.ds(0, 63)]
    tops_in = pltpu.make_async_remote_copy(
        src_ref=everyone,
        dst_ref=everyone,
        send_sem=top_sem.at[0],
        recv_sem=top_sem.at[1],
        device_id=other_core,
        device_id_type=MESH,
    )
    tops_in.wait_recv()
    best = jnp.max(best_of[...], axis=0) - col_norm[pl.ds((zh * 2 + c) * 4 + b, 1), :]
    out = jnp.zeros((1, PIECE), jnp.float32)
    for i in range(RING):
        out = jnp.where(a == i, best[:, i * PIECE : (i + 1) * PIECE], out)
    col_ref[...] = out

    tops_in.wait_send()


def local(sources, targets):
    f32, bf16 = jnp.float32, jnp.bfloat16
    dma = pltpu.SemaphoreType.DMA
    row_best, col_best = pl.pallas_call(
        kernel,
        out_shape=(
            jax.ShapeDtypeStruct((8, LANES), f32),
            jax.ShapeDtypeStruct((1, PIECE), f32),
        ),
        in_specs=[pl.BlockSpec(memory_space=pl.ANY)] * 2,
        out_specs=(pl.BlockSpec(memory_space=pltpu.VMEM),) * 2,
        scratch_shapes=[
            pltpu.VMEM((ROWS, DEPTH), bf16),
            pltpu.VMEM((PIECE, DEPTH), bf16),
            pltpu.VMEM((2, 2, RING, RING, PIECE, DEPTH), bf16),
            pltpu.VMEM((8, ROWS, 2 * LANES), f32),
            pltpu.VMEM((ROWS, LANES), f32),
            pltpu.VMEM((ROWS, LANES), f32),
            pltpu.VMEM((16, 8, LANES), f32),
            pltpu.VMEM((8, 16, LANES), f32),
            pltpu.VMEM((8, 16, LANES), f32),
            pltpu.VMEM((16, 1, LANES), f32),
            pltpu.VMEM((64, 1, LANES), f32),
            pltpu.VMEM((4, 8, LANES), f32),
            pltpu.VMEM((4, 8, LANES), f32),
            pltpu.VMEM((16, LANES), f32),
            pltpu.VMEM((8, LANES), f32),
            dma((2,)),
            dma((48,)),
            dma((8,)),
            dma((55,)),
            dma((20,)),
            dma((20,)),
            dma((2,)),
        ],
        compiler_params=pltpu.CompilerParams(
            collective_id=0, has_side_effects=True, vmem_limit_bytes=55193 * 1024
        ),
        cost_estimate=pl.CostEstimate(
            flops=2 * ROWS * 2048 * DEPTH, bytes_accessed=1 << 22, transcendentals=1 << 21
        ),
    )(sources, targets)
    return row_best.reshape(ROWS), col_best.reshape(PIECE)


def solution(mesh):
    in_specs = (P("src", None), P(("src", "tgt"), None))
    out_specs = (P("src"), P(("src", "tgt")))
    return jax.shard_map(local, mesh=mesh, in_specs=in_specs, out_specs=out_specs, check_vma=False)
```
